32 devices in a mesh: row: 4 (over y, x), rhs: 8 (over z, core).
Axes of the slice: x: 2, y: 2, z: 4, core: 2. Of those that a mesh axis runs over, the one named last changes fastest.
Arguments:
- factor: bfloat16 [2, 2048, 512], P(None, 'row', 'rhs'), may hold values from -0.25 to 0.25
- pivots: float32 [2, 512], replicated, may hold values from 2 to 3
- right_sides: float32 [2048, 1024], P('row', 'rhs'), may hold values from -6 to 6
Outputs:
- solved: float32 [2048, 1024], P('row', 'rhs')
The draws below stay inside these ranges and needn't reach their ends.
All inputs are finite; a program needn't handle non-finite values.
Results may differ from the reference program's by a relative error of at most 0.0003.
Values may be sent and summed in bfloat16 or wider, within the bound.
A program may use at most 64 MiB of HBM per device.

```python
import jax
import jax.numpy as jnp
from jax import lax

NB = 512
PANELS = 2
M = 2048
RHS = 1024


def block_scale(own_key, extent, shards, smallest, top_value):
    level = 1.0
    for position, blocks in shards:
        steps = jax.random.uniform(jax.random.fold_in(jax.random.fold_in(own_key, 6), position), (blocks,), jnp.float32, smallest / len(shards), top_value / len(shards))
        level = level * jnp.repeat(jnp.exp(steps), extent[position] // blocks).reshape((-1,) + (1,) * (len(extent) - 1 - position))
    return level


def normal_values(key, shape, width, bound, pieces=(), dtype=jnp.bfloat16):
    level = block_scale(key, shape, pieces, -0.22, 0.18) if pieces else 1.0
    array = jax.random.normal(key, shape, jnp.float32) * width * level
    return jnp.minimum(jnp.maximum(array, -bound), bound).astype(dtype)


def setup_inputs(seed: int = 0) -> dict:
    arg_keys = jax.random.split(jax.random.key(seed), 4)
    return {
        "factor": normal_values(arg_keys[0], (PANELS, M, NB), (PANELS * NB * 4 // 9) ** -0.5, 0.25, ((1, 4), (2, 8))),
        "pivots": jnp.clip(jax.random.uniform(arg_keys[1], (PANELS, NB), jnp.float32, 2.0, 3.0), 2.0, 3.0),
        "right_sides": normal_values(arg_keys[2], (M, RHS), 1.0, 6.0, ((0, 4), (1, 8)), jnp.float32),
    }


def reference(factor, pivots, right_sides):
    work = right_sides.astype(jnp.float32)
    for k in range(PANELS):
        low = k * NB
        high = low + NB
        block = factor[k][low:high].astype(jnp.float32)
        diag_k = jnp.tril(block, -1) + jnp.diag(pivots[k])
        x_k = lax.linalg.triangular_solve(diag_k, work[low:high], left_side=True, lower=True)
        work = work.at[low:high].set(x_k)
        below = factor[k][high:].astype(jnp.float32)
        update = jnp.dot(below.astype(jnp.float32), x_k.astype(jnp.float32), precision=lax.Precision.HIGHEST, preferred_element_type=jnp.float32)
        work = work.at[high:].add(-update)
    return work
```

```python
import functools

import jax
import jax.numpy as jnp
from jax import lax
from jax.experimental import pallas as pl
from jax.experimental.pallas import tpu as pltpu
from jax.sharding import PartitionSpec as P

F32 = jnp.float32
BF16 = jnp.bfloat16
CORES = 2
LANES = 128
BASE = 16


def dot(a, b):
    return jnp.dot(a, b, preferred_element_type=F32)


def split(a):
    high = a.astype(BF16)
    return high, (a - high.astype(F32)).astype(BF16)


def product(a, b):
    return dot(a[0], b[0]) + (dot(a[1], b[0]) + dot(a[0], b[1]))


def corner(left, middle, right):
    return -product(split(product(left, split(middle))), right)


def invert_tile(tile):
    size = tile.shape[0]
    down = lax.broadcasted_iota(jnp.int32, tile.shape, 0)
    across = lax.broadcasted_iota(jnp.int32, tile.shape, 1)
    span = min(BASE, size)
    near = jnp.where(down // span == across // span, tile, 0.0)
    inverse = jnp.where(down == across, 1.0, 0.0) - near
    power = split(near)
    reach = 2
    while reach < span:
        power = split(product(power, power))
        inverse = inverse + product(split(inverse), power)
        reach *= 2
    while span < size:
        wide = 2 * span
        edge = jnp.where((down // wide == across // wide) & (down // span != across // span), tile, 0.0)
        parts = split(inverse)
        inverse = inverse + corner(parts, edge, parts)
        span = wide
    return inverse


def invert(factor_t, pivot_row, high_ref, low_ref):
    width = factor_t.shape[0]
    down = lax.broadcasted_iota(jnp.int32, (width, width), 0)
    across = lax.broadcasted_iota(jnp.int32, (width, width), 1)
    unit = jnp.where(across > down, factor_t, 0.0) / pivot_row
    size = min(LANES, width)
    blocks = [invert_tile(unit[at : at + size, at : at + size]) for at in range(0, width, size)]
    while size < width:
        joined = []
        for index in range(0, len(blocks), 2):
            at = index * size
            first, second = blocks[index], blocks[index + 1]
            edge = corner(split(first), unit[at : at + size, at + size : at + 2 * size], split(second))
            top = jnp.concatenate([first, edge], axis=1)
            bottom = jnp.concatenate([jnp.zeros_like(first), second], axis=1)
            joined.append(jnp.concatenate([top, bottom], axis=0))
        blocks = joined
        size *= 2
    high, low = split(blocks[0])
    high_ref[...] = high
    low_ref[...] = low


def kernel(
    n_row, n_rhs, parts,
    factor_ref, pivot_ref, right_ref, out_ref,
    panels, solved, work, high_ref, low_ref,
    far_send, far_recv, near_send, near_recv, x_send, x_recv,
):
    count, rows, slab = factor_ref.shape
    n_chip = n_rhs // CORES
    bits = [b for b in range(n_row.bit_length()) if 2**b < n_row]
    piece = right_ref.shape[1] // parts
    row, col = lax.axis_index("row"), lax.axis_index("rhs")
    chip, core = col // CORES, col % CORES
    sibling = col + 1 - 2 * core

    def flip(b):
        return row + (1 - 2 * ((row // 2**b) % 2)) * 2**b

    def peer(d):
        return lax.rem(chip + d, n_chip) * CORES + core

    barrier = pltpu.get_barrier_semaphore()
    partners = [{"rhs": peer(d)} for d in range(1, n_chip)] + [{"rhs": sibling}] + [{"row": flip(b)} for b in bits]
    for partner in partners:
        pl.semaphore_signal(barrier, inc=1, device_id=partner, device_id_type=pl.DeviceIdType.MESH)

    def place(owner):
        return pl.ds(pl.multiple_of(owner * slab, slab), slab)

    for k in range(count):
        panels[k, place(col), :] = factor_ref[k].astype(F32).T.astype(panels.dtype)
    pl.semaphore_wait(barrier, len(partners))

    def remote(src, dst, send, recv, target):
        return pltpu.make_async_remote_copy(
            src_ref=src, dst_ref=dst, send_sem=send, recv_sem=recv, device_id=target, device_id_type=pl.DeviceIdType.MESH
        )

    def far(k, d):
        ref = panels.at[k, place(col), :]
        return remote(ref, ref, far_send.at[k, d], far_recv.at[k, d], {"rhs": peer(d)})

    def near(k, d):
        ref = panels.at[k, place(lax.rem(chip + n_chip - d, n_chip) * CORES + core), :]
        return remote(ref, ref, near_send.at[k, d], near_recv.at[k, d], {"rhs": sibling})

    for k in range(count):

        @pl.when(row >= k)
        def _():
            for d in range(1, n_chip):
                far(k, d).start()
            near(k, 0).start()

    work[...] = right_ref[...].T

    for k in range(count):

        @pl.when(row >= k)
        def _():
            for d in range(1, n_chip):
                far(k, d).wait_recv()
                near(k, d).start()

    for k in range(count):

        @pl.when(row >= k)
        def _():
            for d in range(n_chip):
                near(k, d).wait_recv()

    @pl.when(row < count)
    def _():
        invert(panels[row].astype(F32), pivot_ref[pl.ds(row, 1), :], high_ref, low_ref)

    def part_rows(p):
        return pl.ds(p * piece, piece)

    def send(k, p, b):
        ref = solved.at[k, :, part_rows(p), :]
        return remote(ref, ref, x_send.at[k, p, b], x_recv.at[k, p], {"row": flip(b)})

    def takes(k, b):
        go = row >= 0
        for low in range(b + 1):
            go = jnp.logical_and(go, (row // 2**low) % 2 == (k // 2**low) % 2)
        if b == 0:
            go = jnp.logical_and(go, flip(b) > k)
        return go

    def pass_on(k, p):
        for b in reversed(bits):

            @pl.when(takes(k, b))
            def _():
                send(k, p, b).start()

    def step(k, p):
        at = part_rows(p)

        @pl.when(row == k)
        def _():
            right = split(work[at, :] / pivot_ref[k : k + 1, :])
            x = product(right, (high_ref[...], low_ref[...]))
            work[at, :] = x
            solved[k, 0, at, :], solved[k, 1, at, :] = split(x)
            pass_on(k, p)

        leaf = (row // 1) % 2 != k % 2

        @pl.when(jnp.logical_or(row > k, jnp.logical_and(row < k, jnp.logical_not(leaf))))
        def _():
            send(k, p, 0).wait_recv()
            pass_on(k, p)

        @pl.when(row > k)
        def _():
            panel = panels[k].astype(BF16)
            work[at, :] -= dot(solved[k, 0, at, :], panel) + dot(solved[k, 1, at, :], panel)

    @pl.when(row < count)
    def _():
        for p in range(parts):
            for k in range(count):
                step(k, p)

    @pl.when(row >= count)
    def _():
        for k in range(count):
            for p in range(parts):
                step(k, p)

    out_ref[...] = work[...].T

    for k in range(count):

        @pl.when(row >= k)
        def _():
            for d in range(1, n_chip):
                far(k, d).wait_send()
            for d in range(n_chip):
                near(k, d).wait_send()

        for b in bits:

            @pl.when(takes(k, b))
            def _():
                for p in range(parts):
                    send(k, p, b).wait_send()


def body(n_row, n_rhs, factor, pivots, right_sides):
    count, rows, slab = factor.shape
    width = pivots.shape[1]
    columns = right_sides.shape[1]
    assert rows == width and n_rhs % CORES == 0
    parts = 2
    n_chip = n_rhs // CORES
    n_bits = max(1, (n_row - 1).bit_length())
    wire = BF16 if slab % 16 == 0 else F32
    vmem = pl.BlockSpec(memory_space=pltpu.VMEM)
    dma = pltpu.SemaphoreType.DMA
    return pl.pallas_call(
        functools.partial(kernel, n_row, n_rhs, parts),
        out_shape=jax.ShapeDtypeStruct(right_sides.shape, F32),
        in_specs=[vmem] * 3,
        out_specs=vmem,
        scratch_shapes=[
            pltpu.VMEM((count, width, rows), wire),
            pltpu.VMEM((count, 2, columns, width), BF16),
            pltpu.VMEM((columns, rows), F32),
            pltpu.VMEM((width, width), BF16),
            pltpu.VMEM((width, width), BF16),
            dma((count, n_chip)),
            dma((count, n_chip)),
            dma((count, n_chip)),
            dma((count, n_chip)),
            dma((count, parts, n_bits)),
            dma((count, parts)),
        ],
        compiler_params=pltpu.CompilerParams(collective_id=0, has_side_effects=True, vmem_limit_bytes=40 * 2**20),
    )(factor, pivots, right_sides)


def solution(mesh):
    in_specs = (P(None, "row", "rhs"), P(), P("row", "rhs"))
    out_specs = P("row", "rhs")
    part = functools.partial(body, mesh.shape["row"], mesh.shape["rhs"])
    return jax.shard_map(part, mesh=mesh, in_specs=in_specs, out_specs=out_specs, check_vma=False)
```

```python
import functools

import jax
import jax.numpy as jnp
from jax import lax
from jax.experimental import pallas as pl
from jax.experimental.pallas import tpu as pltpu
from jax.sharding import PartitionSpec as P

F32 = jnp.float32
BF16 = jnp.bfloat16
CORES = 2
LANES = 128
BASE = 16


def dot(a, b):
    return jnp.dot(a, b, preferred_element_type=F32)


def split(a):
    high = a.astype(BF16)
    return high, (a - high.astype(F32)).astype(BF16)


def product(a, b):
    return dot(a[0], b[0]) + (dot(a[1], b[0]) + dot(a[0], b[1]))


def corner(left, middle, right):
    inner = dot(left[0], middle) + dot(left[1], middle)
    return split(-product(split(inner), right))


def invert_tile(tile):
    size = tile.shape[0]
    down = lax.broadcasted_iota(jnp.int32, tile.shape, 0)
    across = lax.broadcasted_iota(jnp.int32, tile.shape, 1)
    span = min(BASE, size)
    near = jnp.where(down // span == across // span, tile, 0.0)
    inverse = jnp.where(down == across, 1.0, 0.0) - near
    power = split(near)
    reach = 2
    while reach < span:
        power = split(product(power, power))
        inverse = inverse + product(split(inverse), power)
        reach *= 2
    while span < size:
        wide = 2 * span
        edge = jnp.where((down // wide == across // wide) & (down // span != across // span), tile, 0.0)
        parts = split(inverse)
        inverse = inverse - product(split(product(parts, split(edge))), parts)
        span = wide
    return inverse


def diagonal(tile, pivot_row):
    down = lax.broadcasted_iota(jnp.int32, tile.shape, 0)
    across = lax.broadcasted_iota(jnp.int32, tile.shape, 1)
    pivot_column = jnp.sum(jnp.where(down == across, pivot_row, 0.0), axis=1, keepdims=True)
    unit = jnp.where(across > down, tile.astype(F32), 0.0) / pivot_row
    return split(invert_tile(unit) / pivot_column)


def combine(blocks, panel, out_ref):
    width = panel.shape[0]
    size = width // len(blocks)
    while size < width:
        joined = []
        for index in range(0, len(blocks), 2):
            at = index * size
            first, second = blocks[index], blocks[index + 1]
            edge = corner(first, panel[at : at + size, at + size : at + 2 * size].astype(BF16), second)
            block = []
            for one, other, between in zip(first, second, edge):
                top = jnp.concatenate([one, between], axis=1)
                bottom = jnp.concatenate([jnp.zeros_like(one), other], axis=1)
                block.append(jnp.concatenate([top, bottom], axis=0))
            joined.append(block)
        blocks = joined
        size *= 2
    out_ref[0], out_ref[1] = blocks[0]


def kernel(
    n_row, n_rhs, parts,
    factor_ref, pivot_ref, right_ref, out_ref,
    panels, solved, work, inverse, tiles,
    far_send, far_recv, near_send, near_recv, tile_send, tile_recv, tile_near_send, tile_near_recv, x_send, x_recv,
):
    count, slab, rows = factor_ref.shape
    width = pivot_ref.shape[1]
    n_chip = n_rhs // CORES
    size = tiles.shape[-1]
    spread = CORES * slab == size
    bits = [b for b in range(n_row.bit_length()) if 2**b < n_row]
    piece = right_ref.shape[1] // parts
    row, col = lax.axis_index("row"), lax.axis_index("rhs")
    chip, core = col // CORES, col % CORES
    sibling = col + 1 - 2 * core

    def flip(b):
        return row + (1 - 2 * ((row // 2**b) % 2)) * 2**b

    def peer(d):
        return lax.rem(chip + d, n_chip) * CORES + core

    barrier = pltpu.get_barrier_semaphore()
    partners = [{"rhs": peer(d)} for d in range(1, n_chip)] + [{"rhs": sibling}] + [{"row": flip(b)} for b in bits]
    for partner in partners:
        pl.semaphore_signal(barrier, inc=1, device_id=partner, device_id_type=pl.DeviceIdType.MESH)

    def place(owner):
        return pl.ds(pl.multiple_of(owner * slab, slab), slab)

    for k in range(count):
        panels[k, place(col), :] = factor_ref[k].astype(panels.dtype)
    pl.semaphore_wait(barrier, len(partners))

    def remote(src, dst, send, recv, target):
        return pltpu.make_async_remote_copy(
            src_ref=src, dst_ref=dst, send_sem=send, recv_sem=recv, device_id=target, device_id_type=pl.DeviceIdType.MESH
        )

    def far(k, d):
        ref = panels.at[k, place(col), :]
        return remote(ref, ref, far_send.at[k, d], far_recv.at[k, d], {"rhs": peer(d)})

    def near(k, d):
        ref = panels.at[k, place(lax.rem(chip + n_chip - d, n_chip) * CORES + core), :]
        return remote(ref, ref, near_send.at[k, d], near_recv.at[k, d], {"rhs": sibling})

    def row_pivots(at):
        return sum(jnp.where(row == k, pivot_ref[k : k + 1, at : at + size], 0.0) for k in range(count))

    def own_pivots():
        return sum(jnp.where(chip == at // size, row_pivots(at), 0.0) for at in range(0, width, size))

    def far_tile(d):
        ref = tiles.at[chip, :, place_half(), :]
        return remote(ref, ref, tile_send.at[d], tile_recv.at[d], {"rhs": peer(d)})

    def near_tile(d):
        ref = tiles.at[lax.rem(chip + n_chip - d, n_chip), :, place_half(), :]
        return remote(ref, ref, tile_near_send.at[d], tile_near_recv.at[d], {"rhs": sibling})

    def place_half():
        return pl.ds(pl.multiple_of(core * (size // CORES), size // CORES), size // CORES)

    def launch(k):
        for d in range(1, n_chip):
            far(k, d).start()
        near(k, 0).start()

    @pl.when(row < count)
    def _():
        launch(row)

    for k in range(count):

        @pl.when(row > k)
        def _():
            launch(k)

    work[...] = right_ref[...].T

    if spread:

        @pl.when(row < count)
        def _():
            near(row, 0).wait_recv()
            at = pl.ds(pl.multiple_of(chip * size, size), size)
            tiles[chip, 0], tiles[chip, 1] = diagonal(panels[row, at, at], own_pivots())
            for d in range(1, n_chip):
                far_tile(d).start()

    def relay(k):
        for d in range(1, n_chip):
            far(k, d).wait_recv()
            near(k, d).start()

    def settle(k, first):
        for d in range(first, n_chip):
            near(k, d).wait_recv()

    @pl.when(row < count)
    def _():
        relay(row)

    for k in range(count):

        @pl.when(row > k)
        def _():
            relay(k)

    @pl.when(row < count)
    def _():
        if spread:
            for d in range(1, n_chip):
                far_tile(d).wait_recv()
                near_tile(d).start()
            settle(row, 1)
            for d in range(1, n_chip):
                near_tile(d).wait_recv()
            panel = panels[row]
            blocks = [(tiles[at, 0], tiles[at, 1]) for at in range(n_chip)]
        else:
            settle(row, 0)
            panel = panels[row]
            blocks = []
            for at in range(0, width, size):
                whole = slice(at, at + size)
                blocks.append(diagonal(panel[whole, whole], row_pivots(at)))
        combine(blocks, panel, inverse)

    for k in range(count):

        @pl.when(row > k)
        def _():
            settle(k, 0)

    def part_rows(p):
        return pl.ds(p * piece, piece)

    def send(k, p, b):
        ref = solved.at[k, :, part_rows(p), :]
        return remote(ref, ref, x_send.at[k, p, b], x_recv.at[k, p], {"row": flip(b)})

    def takes(k, b):
        go = row >= 0
        for low in range(b + 1):
            go = jnp.logical_and(go, (row // 2**low) % 2 == (k // 2**low) % 2)
        if b == 0:
            go = jnp.logical_and(go, flip(b) > k)
        return go

    def pass_on(k, p):
        for b in reversed(bits):

            @pl.when(takes(k, b))
            def _():
                send(k, p, b).start()

    def step(k, p):
        at = part_rows(p)

        @pl.when(row == k)
        def _():
            x = product(split(work[at, :]), (inverse[0], inverse[1]))
            work[at, :] = x
            solved[k, 0, at, :], solved[k, 1, at, :] = split(x)
            pass_on(k, p)

        leaf = (row // 1) % 2 != k % 2

        @pl.when(jnp.logical_or(row > k, jnp.logical_and(row < k, jnp.logical_not(leaf))))
        def _():
            send(k, p, 0).wait_recv()
            pass_on(k, p)

        @pl.when(row > k)
        def _():
            panel = panels[k].astype(BF16)
            work[at, :] -= dot(solved[k, 0, at, :], panel) + dot(solved[k, 1, at, :], panel)

    @pl.when(row < count)
    def _():
        for p in range(parts):
            for k in range(count):
                step(k, p)

    @pl.when(row >= count)
    def _():
        for k in range(count):
            for p in range(parts):
                step(k, p)

    out_ref[...] = work[...].T

    for k in range(count):

        @pl.when(row >= k)
        def _():
            for d in range(1, n_chip):
                far(k, d).wait_send()
            for d in range(n_chip):
                near(k, d).wait_send()

        if spread:

            @pl.when(row == k)
            def _():
                for d in range(1, n_chip):
                    far_tile(d).wait_send()
                    near_tile(d).wait_send()

        for b in bits:

            @pl.when(takes(k, b))
            def _():
                for p in range(parts):
                    send(k, p, b).wait_send()


def body(n_row, n_rhs, factor, pivots, right_sides):
    factor = jnp.swapaxes(factor, 1, 2)
    count, slab, rows = factor.shape
    width = pivots.shape[1]
    columns = right_sides.shape[1]
    assert rows == width and n_rhs % CORES == 0
    parts = 4 if columns % 64 == 0 else 1
    n_chip = n_rhs // CORES
    n_bits = max(1, (n_row - 1).bit_length())
    wire = BF16 if slab % 16 == 0 else F32
    tile = min(LANES, width)
    vmem = pl.BlockSpec(memory_space=pltpu.VMEM)
    dma = pltpu.SemaphoreType.DMA
    return pl.pallas_call(
        functools.partial(kernel, n_row, n_rhs, parts),
        out_shape=jax.ShapeDtypeStruct(right_sides.shape, F32),
        in_specs=[vmem] * 3,
        out_specs=vmem,
        scratch_shapes=[
            pltpu.VMEM((count, width, rows), wire),
            pltpu.VMEM((count, 2, columns, width), BF16),
            pltpu.VMEM((columns, rows), F32),
            pltpu.VMEM((2, width, width), BF16),
            pltpu.VMEM((width // tile, 2, tile, tile), BF16),
            dma((count, n_chip)),
            dma((count, n_chip)),
            dma((count, n_chip)),
            dma((count, n_chip)),
            dma((n_chip,)),
            dma((n_chip,)),
            dma((n_chip,)),
            dma((n_chip,)),
            dma((count, parts, n_bits)),
            dma((count, parts)),
        ],
        compiler_params=pltpu.CompilerParams(collective_id=0, has_side_effects=True, vmem_limit_bytes=40 * 2**20),
    )(factor, pivots, right_sides)


def solution(mesh):
    in_specs = (P(None, "row", "rhs"), P(), P("row", "rhs"))
    out_specs = P("row", "rhs")
    part = functools.partial(body, mesh.shape["row"], mesh.shape["rhs"])
    return jax.shard_map(part, mesh=mesh, in_specs=in_specs, out_specs=out_specs, check_vma=False)
```

```python
import functools

import jax
import jax.numpy as jnp
from jax import lax
from jax.experimental import pallas as pl
from jax.experimental.pallas import tpu as pltpu
from jax.sharding import PartitionSpec as P

F32 = jnp.float32
BF16 = jnp.bfloat16
CORES = 2
LANES = 128
BASE = 16


def dot(a, b):
    return jnp.dot(a, b, preferred_element_type=F32)


def split(a):
    high = a.astype(BF16)
    return high, (a - high.astype(F32)).astype(BF16)


def product(a, b):
    return dot_rows(a, b[0]) + dot(a[0], b[1])


def dot_rows(a, b):
    size = a[0].shape[0]
    both = dot(jnp.concatenate([a[0], a[1]], axis=0), b)
    return both[:size] + both[size:]


def corner(left, middle, right):
    return split(-product(split(dot_rows(left, middle)), right))


def invert_tile(tile):
    size = tile.shape[0]
    down = lax.broadcasted_iota(jnp.int32, tile.shape, 0)
    across = lax.broadcasted_iota(jnp.int32, tile.shape, 1)
    span = min(BASE, size)
    near = jnp.where(down // span == across // span, tile, 0.0)
    inverse = jnp.where(down == across, 1.0, 0.0) - near
    power = split(near)
    reach = 2
    while reach < span:
        power = split(product(power, power))
        inverse = inverse + product(split(inverse), power)
        reach *= 2
    while span < size:
        wide = 2 * span
        edge = jnp.where((down // wide == across // wide) & (down // span != across // span), tile, 0.0)
        parts = split(inverse)
        inverse = inverse - product(split(product(parts, split(edge))), parts)
        span = wide
    return inverse


def diagonal(tile, pivot_row):
    down = lax.broadcasted_iota(jnp.int32, tile.shape, 0)
    across = lax.broadcasted_iota(jnp.int32, tile.shape, 1)
    pivot_column = jnp.sum(jnp.where(down == across, pivot_row, 0.0), axis=1, keepdims=True)
    unit = jnp.where(across > down, tile.astype(F32), 0.0) / pivot_row
    return split(invert_tile(unit) / pivot_column)


def combine(blocks, panel, out_ref):
    width = panel.shape[0]
    size = width // len(blocks)
    while size < width:
        joined = []
        for index in range(0, len(blocks), 2):
            at = index * size
            first, second = blocks[index], blocks[index + 1]
            edge = corner(first, panel[at : at + size, at + size : at + 2 * size].astype(BF16), second)
            block = []
            for one, other, between in zip(first, second, edge):
                top = jnp.concatenate([one, between], axis=1)
                bottom = jnp.concatenate([jnp.zeros_like(one), other], axis=1)
                block.append(jnp.concatenate([top, bottom], axis=0))
            joined.append(block)
        blocks = joined
        size *= 2
    out_ref[0], out_ref[1] = blocks[0]


def kernel(
    n_row, n_rhs, parts,
    factor_hbm, pivot_hbm, right_hbm, out_ref,
    panels, solved, work, inverse, tiles, merged, factor_ref, pivot_ref, right_ref,
    fetch,
    far_send, far_recv, near_send, near_recv, tile_send, tile_recv, tile_near_send, tile_near_recv, x_send, x_recv,
):
    count, slab, rows = factor_ref.shape
    width = pivot_ref.shape[1]
    n_chip = n_rhs // CORES
    size = tiles.shape[-1]
    spread = CORES * slab == size
    bits = [b for b in range(n_row.bit_length()) if 2**b < n_row]
    piece = right_ref.shape[1] // parts
    direct = panels.dtype == factor_hbm.dtype
    row, col = lax.axis_index("row"), lax.axis_index("rhs")
    chip, core = col // CORES, col % CORES
    sibling = col + 1 - 2 * core

    def flip(b):
        return row + (1 - 2 * ((row // 2**b) % 2)) * 2**b

    def peer(d):
        return lax.rem(chip + d, n_chip) * CORES + core

    barrier = pltpu.get_barrier_semaphore()
    partners = [{"rhs": peer(d)} for d in range(1, n_chip)] + [{"rhs": sibling}] + [{"row": flip(b)} for b in bits]
    for partner in partners:
        pl.semaphore_signal(barrier, inc=1, device_id=partner, device_id_type=pl.DeviceIdType.MESH)

    def place(owner):
        return pl.ds(pl.multiple_of(owner * slab, slab), slab)

    def fetched(index, src, dst):
        return pltpu.make_async_copy(src, dst, fetch.at[index])

    in_right = fetched(0, right_hbm, right_ref)
    in_pivot = fetched(1, pivot_hbm, pivot_ref)
    if direct:
        in_factor = [fetched(2 + k, factor_hbm.at[k], panels.at[k, place(col), :]) for k in range(count)]
    else:
        in_factor = [fetched(2 + k, factor_hbm.at[k], factor_ref.at[k]) for k in range(count)]
    for copy in in_factor + [in_right, in_pivot]:
        copy.start()
    if not direct:
        for k in range(count):
            in_factor[k].wait()
            panels[k, place(col), :] = factor_ref[k].astype(panels.dtype)
    pl.semaphore_wait(barrier, len(partners))

    def remote(src, dst, send, recv, target):
        return pltpu.make_async_remote_copy(
            src_ref=src, dst_ref=dst, send_sem=send, recv_sem=recv, device_id=target, device_id_type=pl.DeviceIdType.MESH
        )

    def far(k, d):
        ref = panels.at[k, place(col), :]
        return remote(factor_hbm.at[k] if direct else ref, ref, far_send.at[k, d], far_recv.at[k, d], {"rhs": peer(d)})

    def near(k, d):
        ref = panels.at[k, place(lax.rem(chip + n_chip - d, n_chip) * CORES + core), :]
        return remote(factor_hbm.at[k] if direct and d == 0 else ref, ref, near_send.at[k, d], near_recv.at[k, d], {"rhs": sibling})

    def row_pivots(at):
        return sum(jnp.where(row == k, pivot_ref[k : k + 1, at : at + size], 0.0) for k in range(count))

    def own_pivots():
        return sum(jnp.where(chip == at // size, row_pivots(at), 0.0) for at in range(0, width, size))

    def far_tile(d):
        ref = tiles.at[chip, :, place_half(), :]
        return remote(ref, ref, tile_send.at[d], tile_recv.at[d], {"rhs": peer(d)})

    def near_tile(d):
        ref = tiles.at[lax.rem(chip + n_chip - d, n_chip), :, place_half(), :]
        return remote(ref, ref, tile_near_send.at[d], tile_near_recv.at[d], {"rhs": sibling})

    def place_half():
        return pl.ds(pl.multiple_of(core * (size // CORES), size // CORES), size // CORES)

    def launch(k):
        for d in range(1, n_chip):
            far(k, d).start()
        near(k, 0).start()

    @pl.when(row < count)
    def _():
        launch(row)

    for k in range(count):

        @pl.when(row > k)
        def _():
            launch(k)

    if direct:
        for copy in in_factor:
            copy.wait()
    in_right.wait()
    in_pivot.wait()
    work[...] = right_ref[...].T

    if spread:

        @pl.when(row < count)
        def _():
            near(row, 0).wait_recv()
            at = pl.ds(pl.multiple_of(chip * size, size), size)
            tiles[chip, 0], tiles[chip, 1] = diagonal(panels[row, at, at], own_pivots())
            for d in range(1, n_chip):
                far_tile(d).start()

    def relay(k):
        for d in range(1, n_chip):
            far(k, d).wait_recv()
            near(k, d).start()

    def settle(k, first):
        for d in range(first, n_chip):
            near(k, d).wait_recv()

    @pl.when(row < count)
    def _():
        relay(row)
        if spread:
            for d in range(1, n_chip):
                far_tile(d).wait_recv()
                near_tile(d).start()
            settle(row, 1)
            for d in range(1, n_chip):
                near_tile(d).wait_recv()
            panel = panels[row]
            blocks = [(tiles[at, 0], tiles[at, 1]) for at in range(n_chip)]
        else:
            settle(row, 0)
            panel = panels[row]
            blocks = []
            for at in range(0, width, size):
                whole = slice(at, at + size)
                blocks.append(diagonal(panel[whole, whole], row_pivots(at)))
        combine(blocks, panel, inverse)
        work[...] = product(split(work[...]), (inverse[0], inverse[1]))

    for k in range(count):

        @pl.when(row > k)
        def _():
            relay(k)

    for k in range(count):

        @pl.when(row > k)
        def _():
            settle(k, 0)

        @pl.when(jnp.logical_and(row > k, row < count))
        def _():
            panel = panels[k].astype(BF16)
            merged[k, 0], merged[k, 1] = split(dot(panel, inverse[0]) + dot(panel, inverse[1]))

    def part_rows(p):
        return pl.ds(p * piece, piece)

    def send(k, p, b):
        ref = solved.at[k, :, part_rows(p), :]
        return remote(ref, ref, x_send.at[k, p, b], x_recv.at[k, p], {"row": flip(b)})

    def takes(k, b):
        go = row >= 0
        for low in range(b + 1):
            go = jnp.logical_and(go, (row // 2**low) % 2 == (k // 2**low) % 2)
        if b == 0:
            go = jnp.logical_and(go, flip(b) > k)
        return go

    def pass_on(k, p):
        for b in reversed(bits):

            @pl.when(takes(k, b))
            def _():
                send(k, p, b).start()

    def step(k, p):
        at = part_rows(p)

        @pl.when(row == k)
        def _():
            solved[k, 0, at, :], solved[k, 1, at, :] = split(work[at, :])
            pass_on(k, p)

        leaf = (row // 1) % 2 != k % 2

        @pl.when(jnp.logical_or(row > k, jnp.logical_and(row < k, jnp.logical_not(leaf))))
        def _():
            send(k, p, 0).wait_recv()
            pass_on(k, p)

        @pl.when(jnp.logical_and(row > k, row < count))
        def _():
            work[at, :] -= product((solved[k, 0, at, :], solved[k, 1, at, :]), (merged[k, 0], merged[k, 1]))

        @pl.when(row >= count)
        def _():
            work[at, :] -= dot_rows((solved[k, 0, at, :], solved[k, 1, at, :]), panels[k].astype(BF16))

    @pl.when(row < count)
    def _():
        for p in range(parts):
            for k in range(count):
                step(k, p)

    @pl.when(row >= count)
    def _():
        for k in range(count):
            for p in range(parts):
                step(k, p)

    out_ref[...] = work[...].T

    for k in range(count):

        @pl.when(row >= k)
        def _():
            for d in range(1, n_chip):
                far(k, d).wait_send()
            for d in range(n_chip):
                near(k, d).wait_send()

        if spread:

            @pl.when(row == k)
            def _():
                for d in range(1, n_chip):
                    far_tile(d).wait_send()
                    near_tile(d).wait_send()

        for b in bits:

            @pl.when(takes(k, b))
            def _():
                for p in range(parts):
                    send(k, p, b).wait_send()


def body(n_row, n_rhs, factor, pivots, right_sides):
    factor = jnp.swapaxes(factor, 1, 2)
    count, slab, rows = factor.shape
    width = pivots.shape[1]
    columns = right_sides.shape[1]
    assert rows == width and n_rhs % CORES == 0
    parts = 4 if columns % 64 == 0 else 1
    n_chip = n_rhs // CORES
    n_bits = max(1, (n_row - 1).bit_length())
    wire = BF16 if slab % 16 == 0 else F32
    tile = min(LANES, width)
    vmem = pl.BlockSpec(memory_space=pltpu.VMEM)
    dma = pltpu.SemaphoreType.DMA
    return pl.pallas_call(
        functools.partial(kernel, n_row, n_rhs, parts),
        out_shape=jax.ShapeDtypeStruct(right_sides.shape, F32),
        in_specs=[pl.BlockSpec(memory_space=pl.ANY)] * 3,
        out_specs=vmem,
        scratch_shapes=[
            pltpu.VMEM((count, width, rows), wire),
            pltpu.VMEM((count, 2, columns, width), BF16),
            pltpu.VMEM((columns, rows), F32),
            pltpu.VMEM((2, width, width), BF16),
            pltpu.VMEM((width // tile, 2, tile, tile), BF16),
            pltpu.VMEM((count, 2, width, width), BF16),
            pltpu.VMEM(factor.shape, factor.dtype),
            pltpu.VMEM(pivots.shape, F32),
            pltpu.VMEM(right_sides.shape, F32),
            dma((count + 2,)),
            dma((count, n_chip)),
            dma((count, n_chip)),
            dma((count, n_chip)),
            dma((count, n_chip)),
            dma((n_chip,)),
            dma((n_chip,)),
            dma((n_chip,)),
            dma((n_chip,)),
            dma((count, parts, n_bits)),
            dma((count, parts)),
        ],
        compiler_params=pltpu.CompilerParams(collective_id=0, has_side_effects=True, vmem_limit_bytes=56 * 2**20),
    )(factor, pivots, right_sides)


def solution(mesh):
    in_specs = (P(None, "row", "rhs"), P(), P("row", "rhs"))
    out_specs = P("row", "rhs")
    part = functools.partial(body, mesh.shape["row"], mesh.shape["rhs"])
    return jax.shard_map(part, mesh=mesh, in_specs=in_specs, out_specs=out_specs, check_vma=False)
```

```python
import functools

import jax
import jax.numpy as jnp
from jax import lax
from jax.experimental import pallas as pl
from jax.experimental.pallas import tpu as pltpu
from jax.sharding import PartitionSpec as P

F32 = jnp.float32
BF16 = jnp.bfloat16
CORES = 2
LANES = 128
BASE = 16


def dot(a, b):
    return jnp.dot(a, b, preferred_element_type=F32)


def split(a):
    high = a.astype(BF16)
    return high, (a - high.astype(F32)).astype(BF16)


def product(a, b):
    return dot_rows(a, b[0]) + dot(a[0], b[1])


def dot_rows(a, b):
    size = a[0].shape[0]
    both = dot(jnp.concatenate([a[0], a[1]], axis=0), b)
    return both[:size] + both[size:]


def corner(left, middle, right):
    return split(-product(split(dot_rows(left, middle)), right))


def invert_tile(tile):
    size = tile.shape[0]
    down = lax.broadcasted_iota(jnp.int32, tile.shape, 0)
    across = lax.broadcasted_iota(jnp.int32, tile.shape, 1)
    span = min(BASE, size)
    near = jnp.where(down // span == across // span, tile, 0.0)
    inverse = jnp.where(down == across, 1.0, 0.0) - near
    power = split(near)
    reach = 2
    while reach < span:
        power = split(product(power, power))
        inverse = inverse + product(split(inverse), power)
        reach *= 2
    while span < size:
        wide = 2 * span
        edge = jnp.where((down // wide == across // wide) & (down // span != across // span), tile, 0.0)
        parts = split(inverse)
        inverse = inverse - product(split(product(parts, split(edge))), parts)
        span = wide
    return inverse


def diagonal(tile, pivot_row):
    down = lax.broadcasted_iota(jnp.int32, tile.shape, 0)
    across = lax.broadcasted_iota(jnp.int32, tile.shape, 1)
    pivot_column = jnp.sum(jnp.where(down == across, pivot_row, 0.0), axis=1, keepdims=True)
    unit = jnp.where(across > down, tile.astype(F32), 0.0) / pivot_row
    return split(invert_tile(unit) / pivot_column)


def combine(blocks, width, panel, out_ref):
    size = width // len(blocks)
    while size < width:
        joined = []
        for index in range(0, len(blocks), 2):
            at = index * size
            first, second = blocks[index], blocks[index + 1]
            edge = corner(first, panel(slice(at, at + size), slice(at + size, at + 2 * size)), second)
            block = []
            for one, other, between in zip(first, second, edge):
                top = jnp.concatenate([one, between], axis=1)
                bottom = jnp.concatenate([jnp.zeros_like(one), other], axis=1)
                block.append(jnp.concatenate([top, bottom], axis=0))
            joined.append(block)
        blocks = joined
        size *= 2
    out_ref[0], out_ref[1] = blocks[0]


def kernel(
    n_row, n_rhs, parts,
    factor_hbm, pivot_hbm, right_hbm, out_ref,
    panels, solved, work, inverse, tiles, merged, factor_ref, pivot_ref, right_ref,
    fetch,
    far_send, far_recv, near_send, near_recv, tile_send, tile_recv, tile_near_send, tile_near_recv, x_send, x_recv,
):
    count, slab, rows = factor_ref.shape
    width = pivot_ref.shape[1]
    n_chip = n_rhs // CORES
    size = tiles.shape[-1]
    spread = CORES * slab == size
    bits = [b for b in range(n_row.bit_length()) if 2**b < n_row]
    piece = right_ref.shape[1] // parts
    direct = panels.dtype == factor_hbm.dtype
    row, col = lax.axis_index("row"), lax.axis_index("rhs")
    chip, core = col // CORES, col % CORES
    sibling = col + 1 - 2 * core

    def flip(b):
        return row + (1 - 2 * ((row // 2**b) % 2)) * 2**b

    def peer(d):
        return lax.rem(chip + d, n_chip) * CORES + core

    barrier = pltpu.get_barrier_semaphore()
    partners = [{"rhs": peer(d)} for d in range(1, n_chip)] + [{"rhs": sibling}] + [{"row": flip(b)} for b in bits]
    for partner in partners:
        pl.semaphore_signal(barrier, inc=1, device_id=partner, device_id_type=pl.DeviceIdType.MESH)

    def place(owner):
        return pl.ds(pl.multiple_of(owner * slab, slab), slab)

    def fetched(index, src, dst):
        return pltpu.make_async_copy(src, dst, fetch.at[index])

    in_right = fetched(0, right_hbm, right_ref)
    in_pivot = fetched(1, pivot_hbm, pivot_ref)
    if direct:
        in_factor = [fetched(2 + k, factor_hbm.at[k], panels.at[k, place(col), :]) for k in range(count)]
    else:
        in_factor = [fetched(2 + k, factor_hbm.at[k], factor_ref.at[k]) for k in range(count)]
    for copy in in_factor + [in_right, in_pivot]:
        copy.start()
    if not direct:
        for k in range(count):
            in_factor[k].wait()
            panels[k, place(col), :] = factor_ref[k].astype(panels.dtype)
    pl.semaphore_wait(barrier, len(partners))

    def remote(src, dst, send, recv, target):
        return pltpu.make_async_remote_copy(
            src_ref=src, dst_ref=dst, send_sem=send, recv_sem=recv, device_id=target, device_id_type=pl.DeviceIdType.MESH
        )

    def far(k, d):
        ref = panels.at[k, place(col), :]
        return remote(factor_hbm.at[k] if direct else ref, ref, far_send.at[k, d], far_recv.at[k, d], {"rhs": peer(d)})

    def near(k, d):
        ref = panels.at[k, place(lax.rem(chip + n_chip - d, n_chip) * CORES + core), :]
        return remote(factor_hbm.at[k] if direct and d == 0 else ref, ref, near_send.at[k, d], near_recv.at[k, d], {"rhs": sibling})

    def row_pivots(at):
        return sum(jnp.where(row == k, pivot_ref[k : k + 1, at : at + size], 0.0) for k in range(count))

    def own_pivots():
        return sum(jnp.where(chip == at // size, row_pivots(at), 0.0) for at in range(0, width, size))

    def far_tile(d):
        ref = tiles.at[chip, :, place_half(), :]
        return remote(ref, ref, tile_send.at[d], tile_recv.at[d], {"rhs": peer(d)})

    def near_tile(d):
        ref = tiles.at[lax.rem(chip + n_chip - d, n_chip), :, place_half(), :]
        return remote(ref, ref, tile_near_send.at[d], tile_near_recv.at[d], {"rhs": sibling})

    def place_half():
        return pl.ds(pl.multiple_of(core * (size // CORES), size // CORES), size // CORES)

    def source(d):
        return lax.rem(chip + n_chip - d, n_chip)

    def beyond(c):
        return pl.ds(size * (c + 1), width - size * (c + 1))

    def far_own(c, d):
        src = factor_hbm.at[row, :, beyond(c)] if direct else panels.at[row, place(col), beyond(c)]
        dst = panels.at[row, place(col), beyond(c)]
        return remote(src, dst, far_send.at[row, d], far_recv.at[row, d], {"rhs": peer(d)})

    def near_own(c, d):
        ref = panels.at[row, place(c * CORES + core), beyond(c)]
        return remote(ref, ref, near_send.at[row, d], near_recv.at[row, d], {"rhs": sibling})

    def each_source(act):
        for d in range(1, n_chip):
            for c in range(n_chip - 1):

                @pl.when(source(d) == c)
                def _():
                    act(c, d)

    def launch_own():
        near(row, 0).start()
        if not spread:
            for d in range(1, n_chip):
                far(row, d).start()
            return
        for c in range(n_chip - 1):

            @pl.when(chip == c)
            def _():
                for d in range(1, n_chip):
                    far_own(c, d).start()

    def relay_own():
        if not spread:
            return relay(row)

        def act(c, d):
            far_own(c, d).wait_recv()
            near_own(c, d).start()

        each_source(act)

    def sent_own():
        near(row, 0).wait_send()
        if not spread:
            for d in range(1, n_chip):
                far(row, d).wait_send()
                near(row, d).wait_send()
            return
        for c in range(n_chip - 1):

            @pl.when(chip == c)
            def _():
                for d in range(1, n_chip):
                    far_own(c, d).wait_send()

        each_source(lambda c, d: near_own(c, d).wait_send())

    def launch(k):
        for d in range(1, n_chip):
            far(k, d).start()
        near(k, 0).start()

    @pl.when(row < count)
    def _():
        launch_own()

    @pl.when(row >= count)
    def _():
        for k in range(count):
            launch(k)

    if direct:
        for copy in in_factor:
            copy.wait()
    in_right.wait()
    in_pivot.wait()
    work[...] = right_ref[...].T

    if spread:

        @pl.when(row < count)
        def _():
            near(row, 0).wait_recv()
            at = pl.ds(pl.multiple_of(chip * size, size), size)
            tiles[chip, 0], tiles[chip, 1] = diagonal(panels[row, at, at], own_pivots())
            for d in range(1, n_chip):
                far_tile(d).start()

    def relay(k):
        for d in range(1, n_chip):
            far(k, d).wait_recv()
            near(k, d).start()

    def settle(k):
        for d in range(n_chip):
            near(k, d).wait_recv()

    @pl.when(row < count)
    def _():
        relay_own()
        if spread:
            for d in range(1, n_chip):
                far_tile(d).wait_recv()
                near_tile(d).start()
        for k in range(count - 1):

            @pl.when(row > k)
            def _():
                launch(k)

        if spread:
            each_source(lambda c, d: near_own(c, d).wait_recv())
            for d in range(1, n_chip):
                near_tile(d).wait_recv()
            blocks = [(tiles[at, 0], tiles[at, 1]) for at in range(n_chip)]
        else:
            settle(row)
            blocks = []
            for at in range(0, width, size):
                whole = slice(at, at + size)
                blocks.append(diagonal(panels[row, whole, whole], row_pivots(at)))
        combine(blocks, width, lambda down, across: panels[row, down, across].astype(BF16), inverse)
        work[...] = product(split(work[...]), (inverse[0], inverse[1]))

    for k in range(count):

        @pl.when(row > k)
        def _():
            relay(k)

    for k in range(count):

        @pl.when(row > k)
        def _():
            settle(k)

        @pl.when(jnp.logical_and(row > k, row < count))
        def _():
            panel = panels[k].astype(BF16)
            merged[k, 0], merged[k, 1] = split(dot(panel, inverse[0]) + dot(panel, inverse[1]))

    def part_rows(p):
        return pl.ds(p * piece, piece)

    def send(k, p, b):
        ref = solved.at[k, :, part_rows(p), :]
        return remote(ref, ref, x_send.at[k, p, b], x_recv.at[k, p], {"row": flip(b)})

    def takes(k, b):
        go = row >= 0
        for low in range(b + 1):
            go = jnp.logical_and(go, (row // 2**low) % 2 == (k // 2**low) % 2)
        if b == 0:
            go = jnp.logical_and(go, flip(b) > k)
        return go

    def pass_on(k, p):
        for b in reversed(bits):

            @pl.when(takes(k, b))
            def _():
                send(k, p, b).start()

    def step(k, p):
        at = part_rows(p)

        @pl.when(row == k)
        def _():
            solved[k, 0, at, :], solved[k, 1, at, :] = split(work[at, :])
            pass_on(k, p)

        leaf = (row // 1) % 2 != k % 2

        @pl.when(jnp.logical_or(row > k, jnp.logical_and(row < k, jnp.logical_not(leaf))))
        def _():
            send(k, p, 0).wait_recv()
            pass_on(k, p)

        @pl.when(jnp.logical_and(row > k, row < count))
        def _():
            work[at, :] -= product((solved[k, 0, at, :], solved[k, 1, at, :]), (merged[k, 0], merged[k, 1]))

        @pl.when(row >= count)
        def _():
            work[at, :] -= dot_rows((solved[k, 0, at, :], solved[k, 1, at, :]), panels[k].astype(BF16))

    @pl.when(row < count)
    def _():
        for p in range(parts):
            for k in range(count):
                step(k, p)

    @pl.when(row >= count)
    def _():
        for k in range(count):
            for p in range(parts):
                step(k, p)

    out_ref[...] = work[...].T

    for k in range(count):

        @pl.when(row > k)
        def _():
            for d in range(1, n_chip):
                far(k, d).wait_send()
            for d in range(n_chip):
                near(k, d).wait_send()

        @pl.when(row == k)
        def _():
            sent_own()
            if spread:
                for d in range(1, n_chip):
                    far_tile(d).wait_send()
                    near_tile(d).wait_send()

        for b in bits:

            @pl.when(takes(k, b))
            def _():
                for p in range(parts):
                    send(k, p, b).wait_send()


def body(n_row, n_rhs, factor, pivots, right_sides):
    factor = jnp.swapaxes(factor, 1, 2)
    count, slab, rows = factor.shape
    width = pivots.shape[1]
    columns = right_sides.shape[1]
    assert rows == width and n_rhs % CORES == 0
    parts = 4 if columns % 64 == 0 else 1
    n_chip = n_rhs // CORES
    n_bits = max(1, (n_row - 1).bit_length())
    wire = BF16 if slab % 16 == 0 else F32
    tile = min(LANES, width)
    vmem = pl.BlockSpec(memory_space=pltpu.VMEM)
    dma = pltpu.SemaphoreType.DMA
    return pl.pallas_call(
        functools.partial(kernel, n_row, n_rhs, parts),
        out_shape=jax.ShapeDtypeStruct(right_sides.shape, F32),
        in_specs=[pl.BlockSpec(memory_space=pltpu.HBM)] * 3,
        out_specs=vmem,
        scratch_shapes=[
            pltpu.VMEM((count, width, rows), wire),
            pltpu.VMEM((count, 2, columns, width), BF16),
            pltpu.VMEM((columns, rows), F32),
            pltpu.VMEM((2, width, width), BF16),
            pltpu.VMEM((width // tile, 2, tile, tile), BF16),
            pltpu.VMEM((count, 2, width, width), BF16),
            pltpu.VMEM(factor.shape, factor.dtype),
            pltpu.VMEM(pivots.shape, F32),
            pltpu.VMEM(right_sides.shape, F32),
            dma((count + 2,)),
            dma((count, n_chip)),
            dma((count, n_chip)),
            dma((count, n_chip)),
            dma((count, n_chip)),
            dma((n_chip,)),
            dma((n_chip,)),
            dma((n_chip,)),
            dma((n_chip,)),
            dma((count, parts, n_bits)),
            dma((count, parts)),
        ],
        compiler_params=pltpu.CompilerParams(collective_id=0, has_side_effects=True, vmem_limit_bytes=40 * 2**20),
    )(*[pltpu.with_memory_space_constraint(array, pltpu.HBM) for array in (factor, pivots, right_sides)])


def solution(mesh):
    in_specs = (P(None, "row", "rhs"), P(), P("row", "rhs"))
    out_specs = P("row", "rhs")
    part = functools.partial(body, mesh.shape["row"], mesh.shape["rhs"])
    return jax.shard_map(part, mesh=mesh, in_specs=in_specs, out_specs=out_specs, check_vma=False)
```

```python
import functools

import jax
import jax.numpy as jnp
from jax import lax
from jax.experimental import pallas as pl
from jax.experimental.pallas import tpu as pltpu
from jax.sharding import PartitionSpec as P

F32 = jnp.float32
BF16 = jnp.bfloat16
CORES = 2
LANES = 128
BASE = 16


def dot(a, b):
    return jnp.dot(a, b, preferred_element_type=F32)


def split(a):
    high = a.astype(BF16)
    return high, (a - high.astype(F32)).astype(BF16)


def product(a, b):
    return dot_rows(a, b[0]) + dot(a[0], b[1])


def dot_rows(a, b):
    size = a[0].shape[0]
    both = dot(jnp.concatenate([a[0], a[1]], axis=0), b)
    return both[:size] + both[size:]


def corner(left, middle, right):
    return split(-product(split(dot_rows(left, middle)), right))


def invert_tile(tile):
    size = tile.shape[0]
    down = lax.broadcasted_iota(jnp.int32, tile.shape, 0)
    across = lax.broadcasted_iota(jnp.int32, tile.shape, 1)
    span = min(BASE, size)
    near = jnp.where(down // span == across // span, tile, 0.0)
    inverse = jnp.where(down == across, 1.0, 0.0) - near
    power = split(near)
    reach = 2
    while reach < span:
        power = split(product(power, power))
        inverse = inverse + product(split(inverse), power)
        reach *= 2
    while span < size:
        wide = 2 * span
        edge = jnp.where((down // wide == across // wide) & (down // span != across // span), tile, 0.0)
        parts = split(inverse)
        inverse = inverse - product(split(product(parts, split(edge))), parts)
        span = wide
    return inverse


def diagonal(tile, pivot_row):
    down = lax.broadcasted_iota(jnp.int32, tile.shape, 0)
    across = lax.broadcasted_iota(jnp.int32, tile.shape, 1)
    pivot_column = jnp.sum(jnp.where(down == across, pivot_row, 0.0), axis=1, keepdims=True)
    unit = jnp.where(across > down, tile.astype(F32), 0.0) / pivot_row
    return split(invert_tile(unit) / pivot_column)


def combine(blocks, width, panel, out_ref):
    size = width // len(blocks)
    while size < width:
        joined = []
        for index in range(0, len(blocks), 2):
            at = index * size
            first, second = blocks[index], blocks[index + 1]
            edge = corner(first, panel(slice(at, at + size), slice(at + size, at + 2 * size)), second)
            block = []
            for one, other, between in zip(first, second, edge):
                top = jnp.concatenate([one, between], axis=1)
                bottom = jnp.concatenate([jnp.zeros_like(one), other], axis=1)
                block.append(jnp.concatenate([top, bottom], axis=0))
            joined.append(block)
        blocks = joined
        size *= 2
    out_ref[0], out_ref[1] = blocks[0]


def kernel(
    n_row, n_rhs, parts,
    factor_hbm, pivot_hbm, right_hbm, out_ref,
    panels, solved, work, inverse, tiles, merged, factor_ref, pivot_ref, right_ref,
    fetch,
    far_send, far_recv, near_send, near_recv, tile_send, tile_recv, tile_near_send, tile_near_recv, x_send, x_recv,
):
    count, slab, rows = factor_ref.shape
    width = pivot_ref.shape[1]
    n_chip = n_rhs // CORES
    size = tiles.shape[-1]
    spread = CORES * slab == size
    bits = [b for b in range(n_row.bit_length()) if 2**b < n_row]
    piece = right_ref.shape[1] // parts
    direct = panels.dtype == factor_hbm.dtype
    row, col = lax.axis_index("row"), lax.axis_index("rhs")
    chip, core = col // CORES, col % CORES
    sibling = col + 1 - 2 * core

    def flip(b):
        return row + (1 - 2 * ((row // 2**b) % 2)) * 2**b

    def diagonal_row():
        return flip(0) + flip(1) - row

    def peer(d):
        return lax.rem(chip + d, n_chip) * CORES + core

    barrier = pltpu.get_barrier_semaphore()
    partners = [{"rhs": peer(d)} for d in range(1, n_chip)] + [{"rhs": sibling}] + [{"row": flip(b)} for b in bits]
    if len(bits) > 1:
        partners.append({"row": diagonal_row()})
    for partner in partners:
        pl.semaphore_signal(barrier, inc=1, device_id=partner, device_id_type=pl.DeviceIdType.MESH)

    def place(owner):
        return pl.ds(pl.multiple_of(owner * slab, slab), slab)

    def fetched(index, src, dst):
        return pltpu.make_async_copy(src, dst, fetch.at[index])

    in_right = fetched(0, right_hbm, right_ref)
    in_pivot = fetched(1, pivot_hbm, pivot_ref)
    if direct:
        in_factor = [fetched(2 + k, factor_hbm.at[k], panels.at[k, place(col), :]) for k in range(count)]
    else:
        in_factor = [fetched(2 + k, factor_hbm.at[k], factor_ref.at[k]) for k in range(count)]
    for copy in in_factor + [in_right, in_pivot]:
        copy.start()
    if not direct:
        for k in range(count):
            in_factor[k].wait()
            panels[k, place(col), :] = factor_ref[k].astype(panels.dtype)
    pl.semaphore_wait(barrier, len(partners))

    def remote(src, dst, send, recv, target):
        return pltpu.make_async_remote_copy(
            src_ref=src, dst_ref=dst, send_sem=send, recv_sem=recv, device_id=target, device_id_type=pl.DeviceIdType.MESH
        )

    def far(k, d):
        ref = panels.at[k, place(col), :]
        return remote(factor_hbm.at[k] if direct else ref, ref, far_send.at[k, d], far_recv.at[k, d], {"rhs": peer(d)})

    def near(k, d):
        ref = panels.at[k, place(lax.rem(chip + n_chip - d, n_chip) * CORES + core), :]
        return remote(factor_hbm.at[k] if direct and d == 0 else ref, ref, near_send.at[k, d], near_recv.at[k, d], {"rhs": sibling})

    def row_pivots(at):
        return sum(jnp.where(row == k, pivot_ref[k : k + 1, at : at + size], 0.0) for k in range(count))

    def own_pivots():
        return sum(jnp.where(chip == at // size, row_pivots(at), 0.0) for at in range(0, width, size))

    def far_tile(d):
        ref = tiles.at[chip, :, place_half(), :]
        return remote(ref, ref, tile_send.at[d], tile_recv.at[d], {"rhs": peer(d)})

    def near_tile(d):
        ref = tiles.at[lax.rem(chip + n_chip - d, n_chip), :, place_half(), :]
        return remote(ref, ref, tile_near_send.at[d], tile_near_recv.at[d], {"rhs": sibling})

    def place_half():
        return pl.ds(pl.multiple_of(core * (size // CORES), size // CORES), size // CORES)

    def source(d):
        return lax.rem(chip + n_chip - d, n_chip)

    def beyond(c):
        return pl.ds(size * (c + 1), width - size * (c + 1))

    def far_own(c, d):
        src = factor_hbm.at[row, :, beyond(c)] if direct else panels.at[row, place(col), beyond(c)]
        dst = panels.at[row, place(col), beyond(c)]
        return remote(src, dst, far_send.at[row, d], far_recv.at[row, d], {"rhs": peer(d)})

    def near_own(c, d):
        ref = panels.at[row, place(c * CORES + core), beyond(c)]
        return remote(ref, ref, near_send.at[row, d], near_recv.at[row, d], {"rhs": sibling})

    def each_source(act):
        for d in range(1, n_chip):
            for c in range(n_chip - 1):

                @pl.when(source(d) == c)
                def _():
                    act(c, d)

    def launch_own():
        near(row, 0).start()
        if not spread:
            for d in range(1, n_chip):
                far(row, d).start()
            return
        for c in range(n_chip - 1):

            @pl.when(chip == c)
            def _():
                for d in range(1, n_chip):
                    far_own(c, d).start()

    def relay_own():
        if not spread:
            return relay(row)

        def act(c, d):
            far_own(c, d).wait_recv()
            near_own(c, d).start()

        each_source(act)

    def sent_own():
        near(row, 0).wait_send()
        if not spread:
            for d in range(1, n_chip):
                far(row, d).wait_send()
                near(row, d).wait_send()
            return
        for c in range(n_chip - 1):

            @pl.when(chip == c)
            def _():
                for d in range(1, n_chip):
                    far_own(c, d).wait_send()

        each_source(lambda c, d: near_own(c, d).wait_send())

    def launch(k):
        for d in range(1, n_chip):
            far(k, d).start()
        near(k, 0).start()

    @pl.when(row < count)
    def _():
        launch_own()

    @pl.when(row >= count)
    def _():
        for k in range(count):
            launch(k)

    if direct:
        for copy in in_factor:
            copy.wait()
    in_right.wait()
    in_pivot.wait()
    work[...] = right_ref[...].T

    if spread:

        @pl.when(row < count)
        def _():
            near(row, 0).wait_recv()
            at = pl.ds(pl.multiple_of(chip * size, size), size)
            tiles[chip, 0], tiles[chip, 1] = diagonal(panels[row, at, at], own_pivots())
            for d in range(1, n_chip):
                far_tile(d).start()

    @pl.when(row < count)
    def _():
        for k in range(count - 1):

            @pl.when(row > k)
            def _():
                launch(k)

    def relay(k):
        for d in range(1, n_chip):
            far(k, d).wait_recv()
            near(k, d).start()

    def settle(k):
        for d in range(n_chip):
            near(k, d).wait_recv()

    @pl.when(row < count)
    def _():
        relay_own()
        if spread:
            for d in range(1, n_chip):
                far_tile(d).wait_recv()
                near_tile(d).start()
        if spread:
            each_source(lambda c, d: near_own(c, d).wait_recv())
            for d in range(1, n_chip):
                near_tile(d).wait_recv()
            blocks = [(tiles[at, 0], tiles[at, 1]) for at in range(n_chip)]
        else:
            settle(row)
            blocks = []
            for at in range(0, width, size):
                whole = slice(at, at + size)
                blocks.append(diagonal(panels[row, whole, whole], row_pivots(at)))
        combine(blocks, width, lambda down, across: panels[row, down, across].astype(BF16), inverse)
        work[...] = product(split(work[...]), (inverse[0], inverse[1]))

    for k in range(count):

        @pl.when(row > k)
        def _():
            relay(k)

    for k in range(count):

        @pl.when(row > k)
        def _():
            settle(k)

        @pl.when(jnp.logical_and(row > k, row < count))
        def _():
            panel = panels[k].astype(BF16)
            merged[k, 0], merged[k, 1] = split(dot(panel, inverse[0]) + dot(panel, inverse[1]))

    def part_rows(p):
        return pl.ds(p * piece, piece)

    def send(k, p, b):
        ref = solved.at[k, :, part_rows(p), :]
        return remote(ref, ref, x_send.at[k, p, b], x_recv.at[k, p], {"row": diagonal_row() if b == len(bits) else flip(b)})

    def takes(k, b):
        go = row >= 0
        if b == len(bits):
            if len(bits) < 2 or k < count - 1:
                return None
            for low in range(2):
                go = jnp.logical_and(go, (row // 2**low) % 2 == (k // 2**low) % 2)
            return jnp.logical_and(go, diagonal_row() > k)
        skips = b == 0 and k == count - 1 and len(bits) > 1
        for low in range(2 if skips else b + 1):
            go = jnp.logical_and(go, (row // 2**low) % 2 == (k // 2**low) % 2)
        if b == 0:
            go = jnp.logical_and(go, flip(b) > k)
        return go

    def paths(k):
        return [b for b in [len(bits)] + bits[::-1] if takes(k, b) is not None]

    def pass_on(k, p):
        for b in paths(k):

            @pl.when(takes(k, b))
            def _():
                send(k, p, b).start()

    def step(k, p):
        at = part_rows(p)

        @pl.when(row == k)
        def _():
            solved[k, 0, at, :], solved[k, 1, at, :] = split(work[at, :])
            pass_on(k, p)

        leaf = (row // 1) % 2 != k % 2

        @pl.when(jnp.logical_or(row > k, jnp.logical_and(row < k, jnp.logical_not(leaf))))
        def _():
            send(k, p, 0).wait_recv()
            pass_on(k, p)

        @pl.when(jnp.logical_and(row > k, row < count))
        def _():
            work[at, :] -= product((solved[k, 0, at, :], solved[k, 1, at, :]), (merged[k, 0], merged[k, 1]))

        @pl.when(row >= count)
        def _():
            work[at, :] -= dot_rows((solved[k, 0, at, :], solved[k, 1, at, :]), panels[k].astype(BF16))

    @pl.when(row < count)
    def _():
        for p in range(parts):
            for k in range(count):
                step(k, p)

    @pl.when(row >= count)
    def _():
        for k in range(count):
            for p in range(parts):
                step(k, p)

    out_ref[...] = work[...].T

    for k in range(count):

        @pl.when(row > k)
        def _():
            for d in range(1, n_chip):
                far(k, d).wait_send()
            for d in range(n_chip):
                near(k, d).wait_send()

        @pl.when(row == k)
        def _():
            sent_own()
            if spread:
                for d in range(1, n_chip):
                    far_tile(d).wait_send()
                    near_tile(d).wait_send()

        for b in paths(k):

            @pl.when(takes(k, b))
            def _():
                for p in range(parts):
                    send(k, p, b).wait_send()


def body(n_row, n_rhs, factor, pivots, right_sides):
    factor = jnp.swapaxes(factor, 1, 2)
    count, slab, rows = factor.shape
    width = pivots.shape[1]
    columns = right_sides.shape[1]
    assert rows == width and n_rhs % CORES == 0
    parts = 4 if columns % 64 == 0 else 1
    n_chip = n_rhs // CORES
    n_bits = max(1, (n_row - 1).bit_length())
    wire = BF16 if slab % 16 == 0 else F32
    tile = min(LANES, width)
    vmem = pl.BlockSpec(memory_space=pltpu.VMEM)
    dma = pltpu.SemaphoreType.DMA
    return pl.pallas_call(
        functools.partial(kernel, n_row, n_rhs, parts),
        out_shape=jax.ShapeDtypeStruct(right_sides.shape, F32),
        in_specs=[pl.BlockSpec(memory_space=pltpu.HBM)] * 3,
        out_specs=vmem,
        scratch_shapes=[
            pltpu.VMEM((count, width, rows), wire),
            pltpu.VMEM((count, 2, columns, width), BF16),
            pltpu.VMEM((columns, rows), F32),
            pltpu.VMEM((2, width, width), BF16),
            pltpu.VMEM((width // tile, 2, tile, tile), BF16),
            pltpu.VMEM((count, 2, width, width), BF16),
            pltpu.VMEM(factor.shape, factor.dtype),
            pltpu.VMEM(pivots.shape, F32),
            pltpu.VMEM(right_sides.shape, F32),
            dma((count + 2,)),
            dma((count, n_chip)),
            dma((count, n_chip)),
            dma((count, n_chip)),
            dma((count, n_chip)),
            dma((n_chip,)),
            dma((n_chip,)),
            dma((n_chip,)),
            dma((n_chip,)),
            dma((count, parts, n_bits + 1)),
            dma((count, parts)),
        ],
        compiler_params=pltpu.CompilerParams(collective_id=0, has_side_effects=True, vmem_limit_bytes=40 * 2**20),
    )(*[pltpu.with_memory_space_constraint(array, pltpu.HBM) for array in (factor, pivots, right_sides)])


def solution(mesh):
    in_specs = (P(None, "row", "rhs"), P(), P("row", "rhs"))
    out_specs = P("row", "rhs")
    part = functools.partial(body, mesh.shape["row"], mesh.shape["rhs"])
    return jax.shard_map(part, mesh=mesh, in_specs=in_specs, out_specs=out_specs, check_vma=False)
```

```python
import functools

import jax
import jax.numpy as jnp
from jax import lax
from jax.experimental import pallas as pl
from jax.experimental.pallas import tpu as pltpu
from jax.sharding import PartitionSpec as P

F32 = jnp.float32
BF16 = jnp.bfloat16
CORES = 2
LANES = 128
BASE = 16


def dot(a, b):
    return jnp.dot(a, b, preferred_element_type=F32)


def split(a):
    high = a.astype(BF16)
    return high, (a - high.astype(F32)).astype(BF16)


def product(a, b):
    return dot_rows(a, b[0]) + dot(a[0], b[1])


def dot_rows(a, b):
    size = a[0].shape[0]
    both = dot(jnp.concatenate([a[0], a[1]], axis=0), b)
    return both[:size] + both[size:]


def corner(left, middle, right):
    return split(-product(split(dot_rows(left, middle)), right))


def invert_tile(tile):
    size = tile.shape[0]
    down = lax.broadcasted_iota(jnp.int32, tile.shape, 0)
    across = lax.broadcasted_iota(jnp.int32, tile.shape, 1)
    span = min(BASE, size)
    near = jnp.where(down // span == across // span, tile, 0.0)
    inverse = jnp.where(down == across, 1.0, 0.0) - near
    power = split(near)
    reach = 2
    while reach < span:
        power = split(product(power, power))
        inverse = inverse + product(split(inverse), power)
        reach *= 2
    while span < size:
        wide = 2 * span
        edge = jnp.where((down // wide == across // wide) & (down // span != across // span), tile, 0.0)
        parts = split(inverse)
        inverse = inverse - product(split(product(parts, split(edge))), parts)
        span = wide
    return inverse


def diagonal(tile, pivot_row):
    down = lax.broadcasted_iota(jnp.int32, tile.shape, 0)
    across = lax.broadcasted_iota(jnp.int32, tile.shape, 1)
    pivot_column = jnp.sum(jnp.where(down == across, pivot_row, 0.0), axis=1, keepdims=True)
    unit = jnp.where(across > down, tile.astype(F32), 0.0) / pivot_row
    return split(invert_tile(unit) / pivot_column)


def combine(blocks, width, panel, out_ref):
    size = width // len(blocks)
    while size < width:
        joined = []
        for index in range(0, len(blocks), 2):
            at = index * size
            first, second = blocks[index], blocks[index + 1]
            edge = corner(first, panel(slice(at, at + size), slice(at + size, at + 2 * size)), second)
            block = []
            for one, other, between in zip(first, second, edge):
                top = jnp.concatenate([one, between], axis=1)
                bottom = jnp.concatenate([jnp.zeros_like(one), other], axis=1)
                block.append(jnp.concatenate([top, bottom], axis=0))
            joined.append(block)
        blocks = joined
        size *= 2
    out_ref[0], out_ref[1] = blocks[0]


def kernel(
    n_row, n_rhs, parts,
    factor_hbm, pivot_hbm, right_hbm, out_ref,
    panels, solved, work, inverse, tiles, merged, factor_ref, pivot_ref, right_ref,
    fetch,
    far_send, far_recv, near_send, near_recv, tile_send, tile_recv, tile_near_send, tile_near_recv, x_send, x_recv,
):
    count, slab, rows = factor_ref.shape
    width = pivot_ref.shape[1]
    n_chip = n_rhs // CORES
    size = tiles.shape[-1]
    spread = CORES * slab == size
    bits = [b for b in range(n_row.bit_length()) if 2**b < n_row]
    piece = right_ref.shape[1] // parts
    direct = panels.dtype == factor_hbm.dtype
    row, col = lax.axis_index("row"), lax.axis_index("rhs")
    chip, core = col // CORES, col % CORES
    sibling = col + 1 - 2 * core

    def flip(b):
        return row + (1 - 2 * ((row // 2**b) % 2)) * 2**b

    def diagonal_row():
        return flip(0) + flip(1) - row

    def peer(d):
        return lax.rem(chip + d, n_chip) * CORES + core

    barrier = pltpu.get_barrier_semaphore()
    partners = [{"rhs": peer(d)} for d in range(1, n_chip)] + [{"rhs": sibling}] + [{"row": flip(b)} for b in bits]
    if len(bits) > 1:
        partners.append({"row": diagonal_row()})
    for partner in partners:
        pl.semaphore_signal(barrier, inc=1, device_id=partner, device_id_type=pl.DeviceIdType.MESH)

    def place(owner):
        return pl.ds(pl.multiple_of(owner * slab, slab), slab)

    def fetched(index, src, dst):
        return pltpu.make_async_copy(src, dst, fetch.at[index])

    in_right = fetched(0, right_hbm, right_ref)
    in_pivot = fetched(1, pivot_hbm, pivot_ref)
    if direct:
        in_factor = [fetched(2 + k, factor_hbm.at[k], panels.at[k, place(col), :]) for k in range(count)]
    else:
        in_factor = [fetched(2 + k, factor_hbm.at[k], factor_ref.at[k]) for k in range(count)]
    for copy in in_factor + [in_right, in_pivot]:
        copy.start()
    if not direct:
        for k in range(count):
            in_factor[k].wait()
            panels[k, place(col), :] = factor_ref[k].astype(panels.dtype)
    pl.semaphore_wait(barrier, len(partners))

    def remote(src, dst, send, recv, target):
        return pltpu.make_async_remote_copy(
            src_ref=src, dst_ref=dst, send_sem=send, recv_sem=recv, device_id=target, device_id_type=pl.DeviceIdType.MESH
        )

    def far(k, d):
        ref = panels.at[k, place(col), :]
        return remote(factor_hbm.at[k] if direct else ref, ref, far_send.at[k, d], far_recv.at[k, d], {"rhs": peer(d)})

    def near(k, d):
        ref = panels.at[k, place(lax.rem(chip + n_chip - d, n_chip) * CORES + core), :]
        return remote(factor_hbm.at[k] if direct and d == 0 else ref, ref, near_send.at[k, d], near_recv.at[k, d], {"rhs": sibling})

    def row_pivots(at):
        return sum(jnp.where(row == k, pivot_ref[k : k + 1, at : at + size], 0.0) for k in range(count))

    def own_pivots():
        return sum(jnp.where(chip == at // size, row_pivots(at), 0.0) for at in range(0, width, size))

    def far_tile(d):
        ref = tiles.at[chip, :, place_half(), :]
        return remote(ref, ref, tile_send.at[d], tile_recv.at[d], {"rhs": peer(d)})

    def near_tile(d):
        ref = tiles.at[lax.rem(chip + n_chip - d, n_chip), :, place_half(), :]
        return remote(ref, ref, tile_near_send.at[d], tile_near_recv.at[d], {"rhs": sibling})

    def place_half():
        return pl.ds(pl.multiple_of(core * (size // CORES), size // CORES), size // CORES)

    def source(d):
        return lax.rem(chip + n_chip - d, n_chip)

    def beyond(c):
        return pl.ds(size * (c + 1), width - size * (c + 1))

    def far_own(c, d):
        src = factor_hbm.at[row, :, beyond(c)] if direct else panels.at[row, place(col), beyond(c)]
        dst = panels.at[row, place(col), beyond(c)]
        return remote(src, dst, far_send.at[row, d], far_recv.at[row, d], {"rhs": peer(d)})

    def near_own(c, d):
        ref = panels.at[row, place(c * CORES + core), beyond(c)]
        return remote(ref, ref, near_send.at[row, d], near_recv.at[row, d], {"rhs": sibling})

    def each_source(act):
        for d in range(1, n_chip):
            for c in range(n_chip - 1):

                @pl.when(source(d) == c)
                def _():
                    act(c, d)

    def launch_own():
        near(row, 0).start()
        if not spread:
            for d in range(1, n_chip):
                far(row, d).start()
            return
        for c in range(n_chip - 1):

            @pl.when(chip == c)
            def _():
                for d in range(1, n_chip):
                    far_own(c, d).start()

    def relay_own():
        if not spread:
            return relay(row)

        def act(c, d):
            far_own(c, d).wait_recv()
            near_own(c, d).start()

        each_source(act)

    def sent_own():
        near(row, 0).wait_send()
        if not spread:
            for d in range(1, n_chip):
                far(row, d).wait_send()
                near(row, d).wait_send()
            return
        for c in range(n_chip - 1):

            @pl.when(chip == c)
            def _():
                for d in range(1, n_chip):
                    far_own(c, d).wait_send()

        each_source(lambda c, d: near_own(c, d).wait_send())

    def launch(k):
        for d in range(1, n_chip):
            far(k, d).start()
        near(k, 0).start()

    @pl.when(row < count)
    def _():
        launch_own()

    @pl.when(row >= count)
    def _():
        for k in range(count):
            launch(k)

    if direct:
        for copy in in_factor:
            copy.wait()
    in_right.wait()
    in_pivot.wait()
    work[...] = right_ref[...].T

    if spread:

        @pl.when(row < count)
        def _():
            near(row, 0).wait_recv()
            at = pl.ds(pl.multiple_of(chip * size, size), size)
            tiles[chip, 0], tiles[chip, 1] = diagonal(panels[row, at, at], own_pivots())
            for d in range(1, n_chip):
                far_tile(d).start()

    @pl.when(row < count)
    def _():
        for k in range(count - 1):

            @pl.when(row > k)
            def _():
                launch(k)

    def relay(k):
        for d in range(1, n_chip):
            far(k, d).wait_recv()
            near(k, d).start()

    def settle(k):
        for d in range(n_chip):
            near(k, d).wait_recv()

    @pl.when(row < count)
    def _():
        relay_own()
        if spread:
            for d in range(1, n_chip):
                far_tile(d).wait_recv()
                near_tile(d).start()
        if spread:
            each_source(lambda c, d: near_own(c, d).wait_recv())
            for d in range(1, n_chip):
                near_tile(d).wait_recv()
            blocks = [(tiles[at, 0], tiles[at, 1]) for at in range(n_chip)]
        else:
            settle(row)
            blocks = []
            for at in range(0, width, size):
                whole = slice(at, at + size)
                blocks.append(diagonal(panels[row, whole, whole], row_pivots(at)))
        combine(blocks, width, lambda down, across: panels[row, down, across].astype(BF16), inverse)
        work[...] = product(split(work[...]), (inverse[0], inverse[1]))

    for k in range(count):

        @pl.when(row > k)
        def _():
            relay(k)

    for k in range(count):

        @pl.when(row > k)
        def _():
            settle(k)

        @pl.when(jnp.logical_and(row > k, row < count))
        def _():
            panel = panels[k].astype(BF16)
            merged[k, 0], merged[k, 1] = split(dot(panel, inverse[0]) + dot(panel, inverse[1]))

    def part_rows(p):
        return pl.ds(p * piece, piece)

    def send(k, p, b):
        ref = solved.at[k, :, part_rows(p), :]
        return remote(ref, ref, x_send.at[k, p, b], x_recv.at[k, p], {"row": diagonal_row() if b == len(bits) else flip(b)})

    def skips_stop(k, p):
        return k == count - 1 and len(bits) > 1 and p >= parts // 2

    def takes(k, p, b):
        go = row >= 0
        if b == len(bits):
            if not skips_stop(k, p):
                return None
            for low in range(2):
                go = jnp.logical_and(go, (row // 2**low) % 2 == (k // 2**low) % 2)
            return jnp.logical_and(go, diagonal_row() > k)
        skips = b == 0 and skips_stop(k, p)
        for low in range(2 if skips else b + 1):
            go = jnp.logical_and(go, (row // 2**low) % 2 == (k // 2**low) % 2)
        if b == 0:
            go = jnp.logical_and(go, flip(b) > k)
        return go

    def paths(k, p):
        return [b for b in bits + [len(bits)] if takes(k, p, b) is not None]

    def pass_on(k, p):
        for b in paths(k, p):

            @pl.when(takes(k, p, b))
            def _():
                send(k, p, b).start()

    def step(k, p):
        at = part_rows(p)

        @pl.when(row == k)
        def _():
            solved[k, 0, at, :], solved[k, 1, at, :] = split(work[at, :])
            pass_on(k, p)

        leaf = (row // 1) % 2 != k % 2

        @pl.when(jnp.logical_or(row > k, jnp.logical_and(row < k, jnp.logical_not(leaf))))
        def _():
            send(k, p, 0).wait_recv()
            pass_on(k, p)

        @pl.when(jnp.logical_and(row > k, row < count))
        def _():
            work[at, :] -= product((solved[k, 0, at, :], solved[k, 1, at, :]), (merged[k, 0], merged[k, 1]))

        @pl.when(row >= count)
        def _():
            work[at, :] -= dot_rows((solved[k, 0, at, :], solved[k, 1, at, :]), panels[k].astype(BF16))

    @pl.when(row < count)
    def _():
        for p in range(parts):
            for k in range(count):
                step(k, p)

    @pl.when(row >= count)
    def _():
        for k in range(count):
            for p in range(parts):
                step(k, p)

    out_ref[...] = work[...].T

    for k in range(count):

        @pl.when(row > k)
        def _():
            for d in range(1, n_chip):
                far(k, d).wait_send()
            for d in range(n_chip):
                near(k, d).wait_send()

        @pl.when(row == k)
        def _():
            sent_own()
            if spread:
                for d in range(1, n_chip):
                    far_tile(d).wait_send()
                    near_tile(d).wait_send()

        for p in range(parts):
            for b in paths(k, p):

                @pl.when(takes(k, p, b))
                def _():
                    send(k, p, b).wait_send()


def body(n_row, n_rhs, factor, pivots, right_sides):
    factor = jnp.swapaxes(factor, 1, 2)
    count, slab, rows = factor.shape
    width = pivots.shape[1]
    columns = right_sides.shape[1]
    assert rows == width and n_rhs % CORES == 0
    parts = 4 if columns % 64 == 0 else 1
    n_chip = n_rhs // CORES
    n_bits = max(1, (n_row - 1).bit_length())
    wire = BF16 if slab % 16 == 0 else F32
    tile = min(LANES, width)
    vmem = pl.BlockSpec(memory_space=pltpu.VMEM)
    dma = pltpu.SemaphoreType.DMA
    return pl.pallas_call(
        functools.partial(kernel, n_row, n_rhs, parts),
        out_shape=jax.ShapeDtypeStruct(right_sides.shape, F32),
        in_specs=[pl.BlockSpec(memory_space=pltpu.HBM)] * 3,
        out_specs=vmem,
        scratch_shapes=[
            pltpu.VMEM((count, width, rows), wire),
            pltpu.VMEM((count, 2, columns, width), BF16),
            pltpu.VMEM((columns, rows), F32),
            pltpu.VMEM((2, width, width), BF16),
            pltpu.VMEM((width // tile, 2, tile, tile), BF16),
            pltpu.VMEM((count, 2, width, width), BF16),
            pltpu.VMEM(factor.shape, factor.dtype),
            pltpu.VMEM(pivots.shape, F32),
            pltpu.VMEM(right_sides.shape, F32),
            dma((count + 2,)),
            dma((count, n_chip)),
            dma((count, n_chip)),
            dma((count, n_chip)),
            dma((count, n_chip)),
            dma((n_chip,)),
            dma((n_chip,)),
            dma((n_chip,)),
            dma((n_chip,)),
            dma((count, parts, n_bits + 1)),
            dma((count, parts)),
        ],
        compiler_params=pltpu.CompilerParams(collective_id=0, has_side_effects=True, vmem_limit_bytes=40 * 2**20),
    )(*[pltpu.with_memory_space_constraint(array, pltpu.HBM) for array in (factor, pivots, right_sides)])


def solution(mesh):
    in_specs = (P(None, "row", "rhs"), P(), P("row", "rhs"))
    out_specs = P("row", "rhs")
    part = functools.partial(body, mesh.shape["row"], mesh.shape["rhs"])
    return jax.shard_map(part, mesh=mesh, in_specs=in_specs, out_specs=out_specs, check_vma=False)
```

```python
import functools

import jax
import jax.numpy as jnp
from jax import lax
from jax.experimental import pallas as pl
from jax.experimental.pallas import tpu as pltpu
from jax.sharding import PartitionSpec as P

F32 = jnp.float32
BF16 = jnp.bfloat16
CORES = 2
LANES = 128
BASE = 16


def dot(a, b):
    return jnp.dot(a, b, preferred_element_type=F32)


def split(a):
    high = a.astype(BF16)
    return high, (a - high.astype(F32)).astype(BF16)


def product(a, b):
    return dot_rows(a, b[0]) + dot(a[0], b[1])


def dot_rows(a, b):
    size = a[0].shape[0]
    both = dot(jnp.concatenate([a[0], a[1]], axis=0), b)
    return both[:size] + both[size:]


def corner(left, middle, right):
    return split(-product(split(dot_rows(left, middle)), right))


def invert_tile(tile):
    size = tile.shape[0]
    down = lax.broadcasted_iota(jnp.int32, tile.shape, 0)
    across = lax.broadcasted_iota(jnp.int32, tile.shape, 1)
    span = min(BASE, size)
    near = jnp.where(down // span == across // span, tile, 0.0)
    inverse = jnp.where(down == across, 1.0, 0.0) - near
    power = split(near)
    reach = 2
    while reach < span:
        power = split(product(power, power))
        inverse = inverse + product(split(inverse), power)
        reach *= 2
    while span < size:
        wide = 2 * span
        edge = jnp.where((down // wide == across // wide) & (down // span != across // span), tile, 0.0)
        parts = split(inverse)
        inverse = inverse - product(split(product(parts, split(edge))), parts)
        span = wide
    return inverse


def diagonal(tile, pivot_row):
    down = lax.broadcasted_iota(jnp.int32, tile.shape, 0)
    across = lax.broadcasted_iota(jnp.int32, tile.shape, 1)
    pivot_column = jnp.sum(jnp.where(down == across, pivot_row, 0.0), axis=1, keepdims=True)
    unit = jnp.where(across > down, tile.astype(F32), 0.0) / pivot_row
    return split(invert_tile(unit) / pivot_column)


def combine(blocks, width, panel, out_ref):
    size = width // len(blocks)
    while size < width:
        joined = []
        for index in range(0, len(blocks), 2):
            at = index * size
            first, second = blocks[index], blocks[index + 1]
            edge = corner(first, panel(slice(at, at + size), slice(at + size, at + 2 * size)), second)
            block = []
            for one, other, between in zip(first, second, edge):
                top = jnp.concatenate([one, between], axis=1)
                bottom = jnp.concatenate([jnp.zeros_like(one), other], axis=1)
                block.append(jnp.concatenate([top, bottom], axis=0))
            joined.append(block)
        blocks = joined
        size *= 2
    out_ref[0], out_ref[1] = blocks[0]


def kernel(
    n_row, n_rhs, parts,
    factor_hbm, pivot_hbm, right_hbm, out_ref,
    panels, solved, work, inverse, tiles, merged, factor_ref, pivot_ref, right_ref,
    fetch,
    far_send, far_recv, near_send, near_recv, tile_send, tile_recv, tile_near_send, tile_near_recv, x_send, x_recv,
):
    count, slab, rows = factor_ref.shape
    width = pivot_ref.shape[1]
    n_chip = n_rhs // CORES
    size = tiles.shape[-1]
    spread = CORES * slab == size
    bits = [b for b in range(n_row.bit_length()) if 2**b < n_row]
    piece = right_ref.shape[1] // parts
    direct = panels.dtype == factor_hbm.dtype
    row, col = lax.axis_index("row"), lax.axis_index("rhs")
    chip, core = col // CORES, col % CORES
    sibling = col + 1 - 2 * core

    def flip(b):
        return row + (1 - 2 * ((row // 2**b) % 2)) * 2**b

    def diagonal_row():
        return flip(0) + flip(1) - row

    def peer(d):
        return lax.rem(chip + d, n_chip) * CORES + core

    barrier = pltpu.get_barrier_semaphore()
    partners = [{"rhs": peer(d)} for d in range(1, n_chip)] + [{"rhs": sibling}] + [{"row": flip(b)} for b in bits]
    if len(bits) > 1:
        partners.append({"row": diagonal_row()})
    for partner in partners:
        pl.semaphore_signal(barrier, inc=1, device_id=partner, device_id_type=pl.DeviceIdType.MESH)

    def place(owner):
        return pl.ds(pl.multiple_of(owner * slab, slab), slab)

    def fetched(index, src, dst):
        return pltpu.make_async_copy(src, dst, fetch.at[index])

    in_right = fetched(0, right_hbm, right_ref)
    in_pivot = fetched(1, pivot_hbm, pivot_ref)
    if direct:
        in_factor = [fetched(2 + k, factor_hbm.at[k], panels.at[k, place(col), :]) for k in range(count)]
    else:
        in_factor = [fetched(2 + k, factor_hbm.at[k], factor_ref.at[k]) for k in range(count)]
    for copy in in_factor + [in_right, in_pivot]:
        copy.start()
    if not direct:
        for k in range(count):
            in_factor[k].wait()
            panels[k, place(col), :] = factor_ref[k].astype(panels.dtype)
    pl.semaphore_wait(barrier, len(partners))

    def remote(src, dst, send, recv, target):
        return pltpu.make_async_remote_copy(
            src_ref=src, dst_ref=dst, send_sem=send, recv_sem=recv, device_id=target, device_id_type=pl.DeviceIdType.MESH
        )

    def far(k, d):
        ref = panels.at[k, place(col), :]
        return remote(factor_hbm.at[k] if direct else ref, ref, far_send.at[k, d], far_recv.at[k, d], {"rhs": peer(d)})

    def near(k, d):
        ref = panels.at[k, place(lax.rem(chip + n_chip - d, n_chip) * CORES + core), :]
        return remote(factor_hbm.at[k] if direct and d == 0 else ref, ref, near_send.at[k, d], near_recv.at[k, d], {"rhs": sibling})

    def row_pivots(at):
        return sum(jnp.where(row == k, pivot_ref[k : k + 1, at : at + size], 0.0) for k in range(count))

    def own_pivots():
        return sum(jnp.where(chip == at // size, row_pivots(at), 0.0) for at in range(0, width, size))

    def far_tile(d):
        ref = tiles.at[chip, :, place_half(), :]
        return remote(ref, ref, tile_send.at[d], tile_recv.at[d], {"rhs": peer(d)})

    def near_tile(d):
        ref = tiles.at[lax.rem(chip + n_chip - d, n_chip), :, place_half(), :]
        return remote(ref, ref, tile_near_send.at[d], tile_near_recv.at[d], {"rhs": sibling})

    def place_half():
        return pl.ds(pl.multiple_of(core * (size // CORES), size // CORES), size // CORES)

    def source(d):
        return lax.rem(chip + n_chip - d, n_chip)

    def beyond(c):
        return pl.ds(size * (c + 1), width - size * (c + 1))

    def far_own(c, d):
        src = factor_hbm.at[row, :, beyond(c)] if direct else panels.at[row, place(col), beyond(c)]
        dst = panels.at[row, place(col), beyond(c)]
        return remote(src, dst, far_send.at[row, d], far_recv.at[row, d], {"rhs": peer(d)})

    def near_own(c, d):
        ref = panels.at[row, place(c * CORES + core), beyond(c)]
        return remote(ref, ref, near_send.at[row, d], near_recv.at[row, d], {"rhs": sibling})

    def each_source(act):
        for d in range(1, n_chip):
            for c in range(n_chip - 1):

                @pl.when(source(d) == c)
                def _():
                    act(c, d)

    def launch_own():
        near(row, 0).start()
        if not spread:
            for d in range(1, n_chip):
                far(row, d).start()
            return
        for c in range(n_chip - 1):

            @pl.when(chip == c)
            def _():
                for d in range(1, n_chip):
                    far_own(c, d).start()

    def relay_own():
        if not spread:
            return relay(row)

        def act(c, d):
            far_own(c, d).wait_recv()
            near_own(c, d).start()

        each_source(act)

    def sent_own():
        near(row, 0).wait_send()
        if not spread:
            for d in range(1, n_chip):
                far(row, d).wait_send()
                near(row, d).wait_send()
            return
        for c in range(n_chip - 1):

            @pl.when(chip == c)
            def _():
                for d in range(1, n_chip):
                    far_own(c, d).wait_send()

        each_source(lambda c, d: near_own(c, d).wait_send())

    def launch(k):
        for d in range(1, n_chip):
            far(k, d).start()
        near(k, 0).start()

    @pl.when(row < count)
    def _():
        launch_own()

    @pl.when(row >= count)
    def _():
        for k in range(count):
            launch(k)

    if direct:
        for copy in in_factor:
            copy.wait()
    in_right.wait()
    in_pivot.wait()
    work[...] = right_ref[...].T

    if spread:

        @pl.when(row < count)
        def _():
            near(row, 0).wait_recv()
            at = pl.ds(pl.multiple_of(chip * size, size), size)
            tiles[chip, 0], tiles[chip, 1] = diagonal(panels[row, at, at], own_pivots())
            for d in range(1, n_chip):
                far_tile(d).start()

    @pl.when(row < count)
    def _():
        for k in range(count - 1):

            @pl.when(row > k)
            def _():
                launch(k)

    def relay(k):
        for d in range(1, n_chip):
            far(k, d).wait_recv()
            near(k, d).start()

    def settle(k):
        for d in range(n_chip):
            near(k, d).wait_recv()

    @pl.when(row < count)
    def _():
        relay_own()
        if spread:
            for d in range(1, n_chip):
                far_tile(d).wait_recv()
                near_tile(d).start()
        if spread:
            each_source(lambda c, d: near_own(c, d).wait_recv())
            for d in range(1, n_chip):
                near_tile(d).wait_recv()
            blocks = [(tiles[at, 0], tiles[at, 1]) for at in range(n_chip)]
        else:
            settle(row)
            blocks = []
            for at in range(0, width, size):
                whole = slice(at, at + size)
                blocks.append(diagonal(panels[row, whole, whole], row_pivots(at)))
        combine(blocks, width, lambda down, across: panels[row, down, across].astype(BF16), inverse)
        work[...] = product(split(work[...]), (inverse[0], inverse[1]))

    for k in range(count):

        @pl.when(row > k)
        def _():
            relay(k)

    for k in range(count):

        @pl.when(row > k)
        def _():
            settle(k)

        @pl.when(jnp.logical_and(row > k, row < count))
        def _():
            panel = panels[k].astype(BF16)
            merged[k, 0], merged[k, 1] = split(dot(panel, inverse[0]) + dot(panel, inverse[1]))

    def part_rows(p):
        return pl.ds(p * piece, piece)

    def send(k, p, b):
        ref = solved.at[k, :, part_rows(p), :]
        return remote(ref, ref, x_send.at[k, p, b], x_recv.at[k, p], {"row": diagonal_row() if b == len(bits) else flip(b)})

    def skips_stop(k, p):
        return k == count - 1 and len(bits) > 1 and p > 0

    def takes(k, p, b):
        go = row >= 0
        if b == len(bits):
            if not skips_stop(k, p):
                return None
            for low in range(2):
                go = jnp.logical_and(go, (row // 2**low) % 2 == (k // 2**low) % 2)
            return jnp.logical_and(go, diagonal_row() > k)
        skips = b == 0 and skips_stop(k, p)
        for low in range(2 if skips else b + 1):
            go = jnp.logical_and(go, (row // 2**low) % 2 == (k // 2**low) % 2)
        if b == 0:
            go = jnp.logical_and(go, flip(b) > k)
        return go

    def paths(k, p):
        return [b for b in bits + [len(bits)] if takes(k, p, b) is not None]

    def pass_on(k, p):
        for b in paths(k, p):

            @pl.when(takes(k, p, b))
            def _():
                send(k, p, b).start()

    def step(k, p):
        at = part_rows(p)

        @pl.when(row == k)
        def _():
            solved[k, 0, at, :], solved[k, 1, at, :] = split(work[at, :])
            pass_on(k, p)

        leaf = (row // 1) % 2 != k % 2

        @pl.when(jnp.logical_or(row > k, jnp.logical_and(row < k, jnp.logical_not(leaf))))
        def _():
            send(k, p, 0).wait_recv()
            pass_on(k, p)

        @pl.when(jnp.logical_and(row > k, row < count))
        def _():
            work[at, :] -= product((solved[k, 0, at, :], solved[k, 1, at, :]), (merged[k, 0], merged[k, 1]))

        @pl.when(row >= count)
        def _():
            work[at, :] -= dot_rows((solved[k, 0, at, :], solved[k, 1, at, :]), panels[k].astype(BF16))

    @pl.when(row < count)
    def _():
        for p in range(parts):
            for k in range(count):
                step(k, p)

    @pl.when(jnp.logical_and(row >= count, row % 2 == 0))
    def _():
        for k in range(count):
            for p in range(parts):
                step(k, p)

    @pl.when(jnp.logical_and(row >= count, row % 2 == 1))
    def _():
        pairs = [(k, p) for k in range(count) for p in range(parts)]
        for k, p in sorted(pairs, key=lambda pair: (pair[1] + 2 * pair[0], -pair[0])):
            step(k, p)

    out_ref[...] = work[...].T

    for k in range(count):

        @pl.when(row > k)
        def _():
            for d in range(1, n_chip):
                far(k, d).wait_send()
            for d in range(n_chip):
                near(k, d).wait_send()

        @pl.when(row == k)
        def _():
            sent_own()
            if spread:
                for d in range(1, n_chip):
                    far_tile(d).wait_send()
                    near_tile(d).wait_send()

        for p in range(parts):
            for b in paths(k, p):

                @pl.when(takes(k, p, b))
                def _():
                    send(k, p, b).wait_send()


def body(n_row, n_rhs, factor, pivots, right_sides):
    factor = jnp.swapaxes(factor, 1, 2)
    count, slab, rows = factor.shape
    width = pivots.shape[1]
    columns = right_sides.shape[1]
    assert rows == width and n_rhs % CORES == 0
    parts = 4 if columns % 64 == 0 else 1
    n_chip = n_rhs // CORES
    n_bits = max(1, (n_row - 1).bit_length())
    wire = BF16 if slab % 16 == 0 else F32
    tile = min(LANES, width)
    vmem = pl.BlockSpec(memory_space=pltpu.VMEM)
    dma = pltpu.SemaphoreType.DMA
    return pl.pallas_call(
        functools.partial(kernel, n_row, n_rhs, parts),
        out_shape=jax.ShapeDtypeStruct(right_sides.shape, F32),
        in_specs=[pl.BlockSpec(memory_space=pltpu.HBM)] * 3,
        out_specs=vmem,
        scratch_shapes=[
            pltpu.VMEM((count, width, rows), wire),
            pltpu.VMEM((count, 2, columns, width), BF16),
            pltpu.VMEM((columns, rows), F32),
            pltpu.VMEM((2, width, width), BF16),
            pltpu.VMEM((width // tile, 2, tile, tile), BF16),
            pltpu.VMEM((count, 2, width, width), BF16),
            pltpu.VMEM(factor.shape, factor.dtype),
            pltpu.VMEM(pivots.shape, F32),
            pltpu.VMEM(right_sides.shape, F32),
            dma((count + 2,)),
            dma((count, n_chip)),
            dma((count, n_chip)),
            dma((count, n_chip)),
            dma((count, n_chip)),
            dma((n_chip,)),
            dma((n_chip,)),
            dma((n_chip,)),
            dma((n_chip,)),
            dma((count, parts, n_bits + 1)),
            dma((count, parts)),
        ],
        compiler_params=pltpu.CompilerParams(collective_id=0, has_side_effects=True, vmem_limit_bytes=40 * 2**20),
    )(*[pltpu.with_memory_space_constraint(array, pltpu.HBM) for array in (factor, pivots, right_sides)])


def solution(mesh):
    in_specs = (P(None, "row", "rhs"), P(), P("row", "rhs"))
    out_specs = P("row", "rhs")
    part = functools.partial(body, mesh.shape["row"], mesh.shape["rhs"])
    return jax.shard_map(part, mesh=mesh, in_specs=in_specs, out_specs=out_specs, check_vma=False)
```

```python
import functools

import jax
import jax.numpy as jnp
from jax import lax
from jax.experimental import pallas as pl
from jax.experimental.pallas import tpu as pltpu
from jax.sharding import PartitionSpec as P

F32 = jnp.float32
BF16 = jnp.bfloat16
CORES = 2
LANES = 128
BASE = 16


def dot(a, b):
    return jnp.dot(a, b, preferred_element_type=F32)


def split(a):
    high = a.astype(BF16)
    return high, (a - high.astype(F32)).astype(BF16)


def product(a, b):
    return dot_rows(a, b[0]) + dot(a[0], b[1])


def dot_rows(a, b):
    size = a[0].shape[0]
    both = dot(jnp.concatenate([a[0], a[1]], axis=0), b)
    return both[:size] + both[size:]


def corner(left, middle, right):
    return split(-product(split(dot_rows(left, middle)), right))


def invert_tile(tile):
    size = tile.shape[0]
    down = lax.broadcasted_iota(jnp.int32, tile.shape, 0)
    across = lax.broadcasted_iota(jnp.int32, tile.shape, 1)
    span = min(BASE, size)
    near = jnp.where(down // span == across // span, tile, 0.0)
    inverse = jnp.where(down == across, 1.0, 0.0) - near
    power = split(near)
    reach = 2
    while reach < span:
        power = split(product(power, power))
        inverse = inverse + product(split(inverse), power)
        reach *= 2
    while span < size:
        wide = 2 * span
        edge = jnp.where((down // wide == across // wide) & (down // span != across // span), tile, 0.0)
        parts = split(inverse)
        inverse = inverse - product(split(product(parts, split(edge))), parts)
        span = wide
    return inverse


def diagonal(tile, pivot_row):
    down = lax.broadcasted_iota(jnp.int32, tile.shape, 0)
    across = lax.broadcasted_iota(jnp.int32, tile.shape, 1)
    pivot_column = jnp.sum(jnp.where(down == across, pivot_row, 0.0), axis=1, keepdims=True)
    unit = jnp.where(across > down, tile.astype(F32), 0.0) / pivot_row
    return split(invert_tile(unit) / pivot_column)


def combine(blocks, width, panel, out_ref):
    size = width // len(blocks)
    while size < width:
        joined = []
        for index in range(0, len(blocks), 2):
            at = index * size
            first, second = blocks[index], blocks[index + 1]
            edge = corner(first, panel(slice(at, at + size), slice(at + size, at + 2 * size)), second)
            block = []
            for one, other, between in zip(first, second, edge):
                top = jnp.concatenate([one, between], axis=1)
                bottom = jnp.concatenate([jnp.zeros_like(one), other], axis=1)
                block.append(jnp.concatenate([top, bottom], axis=0))
            joined.append(block)
        blocks = joined
        size *= 2
    out_ref[0], out_ref[1] = blocks[0]


def kernel(
    n_row, n_rhs, parts,
    factor_hbm, pivot_hbm, right_hbm, out_ref,
    panels, solved, work, inverse, tiles, merged, factor_ref, pivot_ref, right_ref,
    fetch,
    far_send, far_recv, near_send, near_recv, tile_send, tile_recv, tile_near_send, tile_near_recv, x_send, x_recv,
):
    count, slab, rows = factor_ref.shape
    width = pivot_ref.shape[1]
    n_chip = n_rhs // CORES
    size = tiles.shape[-1]
    spread = CORES * slab == size
    bits = [b for b in range(n_row.bit_length()) if 2**b < n_row]
    piece = right_ref.shape[1] // parts
    direct = panels.dtype == factor_hbm.dtype
    row, col = lax.axis_index("row"), lax.axis_index("rhs")
    chip, core = col // CORES, col % CORES
    sibling = col + 1 - 2 * core

    def flip(b):
        return row + (1 - 2 * ((row // 2**b) % 2)) * 2**b

    def diagonal_row():
        return flip(0) + flip(1) - row

    def peer(d):
        return lax.rem(chip + d, n_chip) * CORES + core

    barrier = pltpu.get_barrier_semaphore()
    partners = [{"rhs": peer(d)} for d in range(1, n_chip)] + [{"rhs": sibling}] + [{"row": flip(b)} for b in bits]
    if len(bits) > 1:
        partners.append({"row": diagonal_row()})
    for partner in partners:
        pl.semaphore_signal(barrier, inc=1, device_id=partner, device_id_type=pl.DeviceIdType.MESH)

    def place(owner):
        return pl.ds(pl.multiple_of(owner * slab, slab), slab)

    def fetched(index, src, dst):
        return pltpu.make_async_copy(src, dst, fetch.at[index])

    in_right = fetched(0, right_hbm, right_ref)
    in_pivot = fetched(1, pivot_hbm, pivot_ref)
    if direct:
        in_factor = [fetched(2 + k, factor_hbm.at[k], panels.at[k, place(col), :]) for k in range(count)]
    else:
        in_factor = [fetched(2 + k, factor_hbm.at[k], factor_ref.at[k]) for k in range(count)]
    for copy in in_factor + [in_right, in_pivot]:
        copy.start()
    if not direct:
        for k in range(count):
            in_factor[k].wait()
            panels[k, place(col), :] = factor_ref[k].astype(panels.dtype)
    pl.semaphore_wait(barrier, len(partners))

    def remote(src, dst, send, recv, target):
        return pltpu.make_async_remote_copy(
            src_ref=src, dst_ref=dst, send_sem=send, recv_sem=recv, device_id=target, device_id_type=pl.DeviceIdType.MESH
        )

    def far(k, d):
        ref = panels.at[k, place(col), :]
        return remote(factor_hbm.at[k] if direct else ref, ref, far_send.at[k, d], far_recv.at[k, d], {"rhs": peer(d)})

    def near(k, d):
        ref = panels.at[k, place(lax.rem(chip + n_chip - d, n_chip) * CORES + core), :]
        return remote(factor_hbm.at[k] if direct and d == 0 else ref, ref, near_send.at[k, d], near_recv.at[k, d], {"rhs": sibling})

    def row_pivots(at):
        return sum(jnp.where(row == k, pivot_ref[k : k + 1, at : at + size], 0.0) for k in range(count))

    def own_pivots():
        return sum(jnp.where(chip == at // size, row_pivots(at), 0.0) for at in range(0, width, size))

    def far_tile(d):
        ref = tiles.at[chip, :, place_half(), :]
        return remote(ref, ref, tile_send.at[d], tile_recv.at[d], {"rhs": peer(d)})

    def near_tile(d):
        ref = tiles.at[lax.rem(chip + n_chip - d, n_chip), :, place_half(), :]
        return remote(ref, ref, tile_near_send.at[d], tile_near_recv.at[d], {"rhs": sibling})

    def place_half():
        return pl.ds(pl.multiple_of(core * (size // CORES), size // CORES), size // CORES)

    def source(d):
        return lax.rem(chip + n_chip - d, n_chip)

    def beyond(c):
        return pl.ds(size * (c + 1), width - size * (c + 1))

    def far_own(c, d):
        src = factor_hbm.at[row, :, beyond(c)] if direct else panels.at[row, place(col), beyond(c)]
        dst = panels.at[row, place(col), beyond(c)]
        return remote(src, dst, far_send.at[row, d], far_recv.at[row, d], {"rhs": peer(d)})

    def near_own(c, d):
        ref = panels.at[row, place(c * CORES + core), beyond(c)]
        return remote(ref, ref, near_send.at[row, d], near_recv.at[row, d], {"rhs": sibling})

    def each_source(act):
        for d in range(1, n_chip):
            for c in range(n_chip - 1):

                @pl.when(source(d) == c)
                def _():
                    act(c, d)

    def launch_own():
        near(row, 0).start()
        if not spread:
            for d in range(1, n_chip):
                far(row, d).start()
            return
        for c in range(n_chip - 1):

            @pl.when(chip == c)
            def _():
                for d in range(1, n_chip):
                    far_own(c, d).start()

    def relay_own():
        if not spread:
            return relay(row)

        def act(c, d):
            far_own(c, d).wait_recv()
            near_own(c, d).start()

        each_source(act)

    def sent_own():
        near(row, 0).wait_send()
        if not spread:
            for d in range(1, n_chip):
                far(row, d).wait_send()
                near(row, d).wait_send()
            return
        for c in range(n_chip - 1):

            @pl.when(chip == c)
            def _():
                for d in range(1, n_chip):
                    far_own(c, d).wait_send()

        each_source(lambda c, d: near_own(c, d).wait_send())

    def launch(k):
        for d in range(1, n_chip):
            far(k, d).start()
        near(k, 0).start()

    @pl.when(row < count)
    def _():
        launch_own()

    @pl.when(row >= count)
    def _():
        for k in range(count):
            launch(k)

    if direct:
        for copy in in_factor:
            copy.wait()
    in_right.wait()
    in_pivot.wait()
    work[...] = right_ref[...].T

    if spread:

        @pl.when(row < count)
        def _():
            near(row, 0).wait_recv()
            at = pl.ds(pl.multiple_of(chip * size, size), size)
            tiles[chip, 0], tiles[chip, 1] = diagonal(panels[row, at, at], own_pivots())
            for d in range(1, n_chip):
                far_tile(d).start()

    @pl.when(row < count)
    def _():
        for k in range(count - 1):

            @pl.when(row > k)
            def _():
                launch(k)

    def relay(k):
        for d in range(1, n_chip):
            far(k, d).wait_recv()
            near(k, d).start()

    def settle(k):
        for d in range(n_chip):
            near(k, d).wait_recv()

    @pl.when(row < count)
    def _():
        relay_own()
        if spread:
            for d in range(1, n_chip):
                far_tile(d).wait_recv()
                near_tile(d).start()
        if spread:
            each_source(lambda c, d: near_own(c, d).wait_recv())
            for d in range(1, n_chip):
                near_tile(d).wait_recv()
            blocks = [(tiles[at, 0], tiles[at, 1]) for at in range(n_chip)]
        else:
            settle(row)
            blocks = []
            for at in range(0, width, size):
                whole = slice(at, at + size)
                blocks.append(diagonal(panels[row, whole, whole], row_pivots(at)))
        combine(blocks, width, lambda down, across: panels[row, down, across].astype(BF16), inverse)
    for k in range(count):

        @pl.when(row > k)
        def _():
            relay(k)

    @pl.when(jnp.logical_and(row > 0, row < count))
    def _():
        work[...] = product(split(work[...]), (inverse[0], inverse[1]))

    for k in range(count):

        @pl.when(row > k)
        def _():
            settle(k)

        @pl.when(jnp.logical_and(row > k, row < count))
        def _():
            panel = panels[k].astype(BF16)
            merged[k, 0], merged[k, 1] = split(dot(panel, inverse[0]) + dot(panel, inverse[1]))

    def part_rows(p):
        return pl.ds(p * piece, piece)

    def send(k, p, b):
        ref = solved.at[k, :, part_rows(p), :]
        return remote(ref, ref, x_send.at[k, p, b], x_recv.at[k, p], {"row": diagonal_row() if b == len(bits) else flip(b)})

    def skips_stop(k, p):
        return k == count - 1 and len(bits) > 1 and p >= parts // 4

    def takes(k, p, b):
        go = row >= 0
        if b == len(bits):
            if not skips_stop(k, p):
                return None
            for low in range(2):
                go = jnp.logical_and(go, (row // 2**low) % 2 == (k // 2**low) % 2)
            return jnp.logical_and(go, diagonal_row() > k)
        skips = b == 0 and skips_stop(k, p)
        for low in range(2 if skips else b + 1):
            go = jnp.logical_and(go, (row // 2**low) % 2 == (k // 2**low) % 2)
        if b == 0:
            go = jnp.logical_and(go, flip(b) > k)
        return go

    def paths(k, p):
        return [b for b in bits + [len(bits)] if takes(k, p, b) is not None]

    def pass_on(k, p):
        for b in paths(k, p):

            @pl.when(takes(k, p, b))
            def _():
                send(k, p, b).start()

    half = max(1, parts // 2)

    def step(k, p):
        at = part_rows(p)

        @pl.when(row == k)
        def _():
            if k == 0 and p % half == 0:
                group = pl.ds(p * piece, half * piece)
                work[group, :] = product(split(work[group, :]), (inverse[0], inverse[1]))
            solved[k, 0, at, :], solved[k, 1, at, :] = split(work[at, :])
            pass_on(k, p)

        leaf = (row // 1) % 2 != k % 2

        @pl.when(jnp.logical_or(row > k, jnp.logical_and(row < k, jnp.logical_not(leaf))))
        def _():
            send(k, p, 0).wait_recv()
            pass_on(k, p)

        @pl.when(jnp.logical_and(row > k, row < count))
        def _():
            work[at, :] -= product((solved[k, 0, at, :], solved[k, 1, at, :]), (merged[k, 0], merged[k, 1]))

        @pl.when(row >= count)
        def _():
            work[at, :] -= dot_rows((solved[k, 0, at, :], solved[k, 1, at, :]), panels[k].astype(BF16))

    @pl.when(row < count)
    def _():
        for p in range(parts):
            for k in range(count):
                step(k, p)

    @pl.when(jnp.logical_and(row >= count, row % 2 == 0))
    def _():
        for k in range(count):
            for p in range(parts):
                step(k, p)

    @pl.when(jnp.logical_and(row >= count, row % 2 == 1))
    def _():
        pairs = [(k, p) for k in range(count) for p in range(parts)]
        for k, p in sorted(pairs, key=lambda pair: (pair[1] + parts // 2 * pair[0], -pair[0])):
            step(k, p)

    out_ref[...] = work[...].T

    for k in range(count):

        @pl.when(row > k)
        def _():
            for d in range(1, n_chip):
                far(k, d).wait_send()
            for d in range(n_chip):
                near(k, d).wait_send()

        @pl.when(row == k)
        def _():
            sent_own()
            if spread:
                for d in range(1, n_chip):
                    far_tile(d).wait_send()
                    near_tile(d).wait_send()

        for p in range(parts):
            for b in paths(k, p):

                @pl.when(takes(k, p, b))
                def _():
                    send(k, p, b).wait_send()


def body(n_row, n_rhs, factor, pivots, right_sides):
    factor = jnp.swapaxes(factor, 1, 2)
    count, slab, rows = factor.shape
    width = pivots.shape[1]
    columns = right_sides.shape[1]
    assert rows == width and n_rhs % CORES == 0
    parts = max(1, columns // 16)
    n_chip = n_rhs // CORES
    n_bits = max(1, (n_row - 1).bit_length())
    wire = BF16 if slab % 16 == 0 else F32
    tile = min(LANES, width)
    vmem = pl.BlockSpec(memory_space=pltpu.VMEM)
    dma = pltpu.SemaphoreType.DMA
    return pl.pallas_call(
        functools.partial(kernel, n_row, n_rhs, parts),
        out_shape=jax.ShapeDtypeStruct(right_sides.shape, F32),
        in_specs=[pl.BlockSpec(memory_space=pltpu.HBM)] * 3,
        out_specs=vmem,
        scratch_shapes=[
            pltpu.VMEM((count, width, rows), wire),
            pltpu.VMEM((count, 2, columns, width), BF16),
            pltpu.VMEM((columns, rows), F32),
            pltpu.VMEM((2, width, width), BF16),
            pltpu.VMEM((width // tile, 2, tile, tile), BF16),
            pltpu.VMEM((count, 2, width, width), BF16),
            pltpu.VMEM(factor.shape, factor.dtype),
            pltpu.VMEM(pivots.shape, F32),
            pltpu.VMEM(right_sides.shape, F32),
            dma((count + 2,)),
            dma((count, n_chip)),
            dma((count, n_chip)),
            dma((count, n_chip)),
            dma((count, n_chip)),
            dma((n_chip,)),
            dma((n_chip,)),
            dma((n_chip,)),
            dma((n_chip,)),
            dma((count, parts, n_bits + 1)),
            dma((count, parts)),
        ],
        compiler_params=pltpu.CompilerParams(collective_id=0, has_side_effects=True, vmem_limit_bytes=40 * 2**20),
    )(*[pltpu.with_memory_space_constraint(array, pltpu.HBM) for array in (factor, pivots, right_sides)])


def solution(mesh):
    in_specs = (P(None, "row", "rhs"), P(), P("row", "rhs"))
    out_specs = P("row", "rhs")
    part = functools.partial(body, mesh.shape["row"], mesh.shape["rhs"])
    return jax.shard_map(part, mesh=mesh, in_specs=in_specs, out_specs=out_specs, check_vma=False)
```

```python
import functools

import jax
import jax.numpy as jnp
from jax import lax
from jax.experimental import pallas as pl
from jax.experimental.pallas import tpu as pltpu
from jax.sharding import PartitionSpec as P

F32 = jnp.float32
BF16 = jnp.bfloat16
CORES = 2
LANES = 128
BASE = 16


def dot(a, b):
    return jnp.dot(a, b, preferred_element_type=F32)


def split(a):
    high = a.astype(BF16)
    return high, (a - high.astype(F32)).astype(BF16)


def product(a, b):
    return dot_rows(a, b[0]) + dot(a[0], b[1])


def dot_rows(a, b):
    size = a[0].shape[0]
    both = dot(jnp.concatenate([a[0], a[1]], axis=0), b)
    return both[:size] + both[size:]


def corner(left, middle, right):
    return split(-product(split(dot_rows(left, middle)), right))


def invert_tile(tile):
    size = tile.shape[0]
    down = lax.broadcasted_iota(jnp.int32, tile.shape, 0)
    across = lax.broadcasted_iota(jnp.int32, tile.shape, 1)
    span = min(BASE, size)
    near = jnp.where(down // span == across // span, tile, 0.0)
    inverse = jnp.where(down == across, 1.0, 0.0) - near
    power = split(near)
    reach = 2
    while reach < span:
        power = split(product(power, power))
        inverse = inverse + product(split(inverse), power)
        reach *= 2
    while span < size:
        wide = 2 * span
        edge = jnp.where((down // wide == across // wide) & (down // span != across // span), tile, 0.0)
        parts = split(inverse)
        inverse = inverse - product(split(product(parts, split(edge))), parts)
        span = wide
    return inverse


def diagonal(tile, pivot_row):
    down = lax.broadcasted_iota(jnp.int32, tile.shape, 0)
    across = lax.broadcasted_iota(jnp.int32, tile.shape, 1)
    pivot_column = jnp.sum(jnp.where(down == across, pivot_row, 0.0), axis=1, keepdims=True)
    unit = jnp.where(across > down, tile.astype(F32), 0.0) / pivot_row
    return split(invert_tile(unit) / pivot_column)


def combine(blocks, width, panel, out_ref):
    size = width // len(blocks)
    while size < width:
        joined = []
        for index in range(0, len(blocks), 2):
            at = index * size
            first, second = blocks[index], blocks[index + 1]
            edge = corner(first, panel(slice(at, at + size), slice(at + size, at + 2 * size)), second)
            block = []
            for one, other, between in zip(first, second, edge):
                top = jnp.concatenate([one, between], axis=1)
                bottom = jnp.concatenate([jnp.zeros_like(one), other], axis=1)
                block.append(jnp.concatenate([top, bottom], axis=0))
            joined.append(block)
        blocks = joined
        size *= 2
    out_ref[0], out_ref[1] = blocks[0]


def kernel(
    n_row, n_rhs, parts,
    factor_hbm, pivot_hbm, right_hbm, out_ref,
    panels, solved, work, inverse, tiles, merged, factor_ref, pivot_ref, right_ref,
    fetch,
    far_send, far_recv, near_send, near_recv, tile_send, tile_recv, tile_near_send, tile_near_recv, x_send, x_recv,
):
    count, slab, rows = factor_ref.shape
    width = pivot_ref.shape[1]
    n_chip = n_rhs // CORES
    size = tiles.shape[-1]
    spread = CORES * slab == size
    bits = [b for b in range(n_row.bit_length()) if 2**b < n_row]
    piece = right_ref.shape[1] // parts
    direct = panels.dtype == factor_hbm.dtype
    row, col = lax.axis_index("row"), lax.axis_index("rhs")
    chip, core = col // CORES, col % CORES
    sibling = col + 1 - 2 * core

    def flip(b):
        return row + (1 - 2 * ((row // 2**b) % 2)) * 2**b

    def diagonal_row():
        return flip(0) + flip(1) - row

    def peer(d):
        return lax.rem(chip + d, n_chip) * CORES + core

    barrier = pltpu.get_barrier_semaphore()
    partners = [{"rhs": peer(d)} for d in range(1, n_chip)] + [{"rhs": sibling}] + [{"row": flip(b)} for b in bits]
    if len(bits) > 1:
        partners.append({"row": diagonal_row()})
    for partner in partners:
        pl.semaphore_signal(barrier, inc=1, device_id=partner, device_id_type=pl.DeviceIdType.MESH)

    def place(owner):
        return pl.ds(pl.multiple_of(owner * slab, slab), slab)

    def fetched(index, src, dst):
        return pltpu.make_async_copy(src, dst, fetch.at[index])

    in_right = fetched(0, right_hbm, right_ref)
    in_pivot = fetched(1, pivot_hbm, pivot_ref)
    if direct:
        in_factor = [fetched(2 + k, factor_hbm.at[k], panels.at[k, place(col), :]) for k in range(count)]
    else:
        in_factor = [fetched(2 + k, factor_hbm.at[k], factor_ref.at[k]) for k in range(count)]
    for copy in in_factor + [in_right, in_pivot]:
        copy.start()
    if not direct:
        for k in range(count):
            in_factor[k].wait()
            panels[k, place(col), :] = factor_ref[k].astype(panels.dtype)
    pl.semaphore_wait(barrier, len(partners))

    def remote(src, dst, send, recv, target):
        return pltpu.make_async_remote_copy(
            src_ref=src, dst_ref=dst, send_sem=send, recv_sem=recv, device_id=target, device_id_type=pl.DeviceIdType.MESH
        )

    def far(k, d):
        ref = panels.at[k, place(col), :]
        return remote(factor_hbm.at[k] if direct else ref, ref, far_send.at[k, d], far_recv.at[k, d], {"rhs": peer(d)})

    def near(k, d):
        ref = panels.at[k, place(lax.rem(chip + n_chip - d, n_chip) * CORES + core), :]
        return remote(factor_hbm.at[k] if direct and d == 0 else ref, ref, near_send.at[k, d], near_recv.at[k, d], {"rhs": sibling})

    def row_pivots(at):
        return sum(jnp.where(row == k, pivot_ref[k : k + 1, at : at + size], 0.0) for k in range(count))

    def own_pivots():
        return sum(jnp.where(chip == at // size, row_pivots(at), 0.0) for at in range(0, width, size))

    def far_tile(d):
        ref = tiles.at[chip, :, place_half(), :]
        return remote(ref, ref, tile_send.at[d], tile_recv.at[d], {"rhs": peer(d)})

    def near_tile(d):
        ref = tiles.at[lax.rem(chip + n_chip - d, n_chip), :, place_half(), :]
        return remote(ref, ref, tile_near_send.at[d], tile_near_recv.at[d], {"rhs": sibling})

    def place_half():
        return pl.ds(pl.multiple_of(core * (size // CORES), size // CORES), size // CORES)

    def source(d):
        return lax.rem(chip + n_chip - d, n_chip)

    def beyond(c):
        return pl.ds(size * (c + 1), width - size * (c + 1))

    def far_own(c, d):
        src = factor_hbm.at[row, :, beyond(c)] if direct else panels.at[row, place(col), beyond(c)]
        dst = panels.at[row, place(col), beyond(c)]
        return remote(src, dst, far_send.at[row, d], far_recv.at[row, d], {"rhs": peer(d)})

    def near_own(c, d):
        ref = panels.at[row, place(c * CORES + core), beyond(c)]
        return remote(ref, ref, near_send.at[row, d], near_recv.at[row, d], {"rhs": sibling})

    def each_source(act):
        for d in range(1, n_chip):
            for c in range(n_chip - 1):

                @pl.when(source(d) == c)
                def _():
                    act(c, d)

    def launch_own():
        near(row, 0).start()
        if not spread:
            for d in range(1, n_chip):
                far(row, d).start()
            return
        for c in range(n_chip - 1):

            @pl.when(chip == c)
            def _():
                for d in range(1, n_chip):
                    far_own(c, d).start()

    def relay_own():
        if not spread:
            return relay(row)

        def act(c, d):
            far_own(c, d).wait_recv()
            near_own(c, d).start()

        each_source(act)

    def sent_own():
        near(row, 0).wait_send()
        if not spread:
            for d in range(1, n_chip):
                far(row, d).wait_send()
                near(row, d).wait_send()
            return
        for c in range(n_chip - 1):

            @pl.when(chip == c)
            def _():
                for d in range(1, n_chip):
                    far_own(c, d).wait_send()

        each_source(lambda c, d: near_own(c, d).wait_send())

    def launch(k):
        for d in range(1, n_chip):
            far(k, d).start()
        near(k, 0).start()

    @pl.when(row < count)
    def _():
        launch_own()

    @pl.when(row >= count)
    def _():
        for k in range(count):
            launch(k)

    if direct:
        for copy in in_factor:
            copy.wait()
    in_right.wait()
    in_pivot.wait()
    work[...] = right_ref[...].T

    if spread:

        @pl.when(row < count)
        def _():
            near(row, 0).wait_recv()
            at = pl.ds(pl.multiple_of(chip * size, size), size)
            tiles[chip, 0], tiles[chip, 1] = diagonal(panels[row, at, at], own_pivots())
            for d in range(1, n_chip):
                far_tile(d).start()

    @pl.when(row < count)
    def _():
        for k in range(count - 1):

            @pl.when(row > k)
            def _():
                launch(k)

    def relay(k):
        for d in range(1, n_chip):
            far(k, d).wait_recv()
            near(k, d).start()

    def settle(k):
        for d in range(n_chip):
            near(k, d).wait_recv()

    @pl.when(row < count)
    def _():
        relay_own()
        if spread:
            for d in range(1, n_chip):
                far_tile(d).wait_recv()
                near_tile(d).start()
        if spread:
            each_source(lambda c, d: near_own(c, d).wait_recv())
            for d in range(1, n_chip):
                near_tile(d).wait_recv()
            blocks = [(tiles[at, 0], tiles[at, 1]) for at in range(n_chip)]
        else:
            settle(row)
            blocks = []
            for at in range(0, width, size):
                whole = slice(at, at + size)
                blocks.append(diagonal(panels[row, whole, whole], row_pivots(at)))
        combine(blocks, width, lambda down, across: panels[row, down, across].astype(BF16), inverse)
    for k in range(count):

        @pl.when(row > k)
        def _():
            relay(k)

    @pl.when(jnp.logical_and(row > 0, row < count))
    def _():
        work[...] = product(split(work[...]), (inverse[0], inverse[1]))

    for k in range(count):

        @pl.when(row > k)
        def _():
            settle(k)

        @pl.when(jnp.logical_and(row > k, row < count))
        def _():
            panel = panels[k].astype(BF16)
            merged[k, 0], merged[k, 1] = split(dot(panel, inverse[0]) + dot(panel, inverse[1]))

    def part_rows(p):
        return pl.ds(p * piece, piece)

    def send(k, p, b):
        ref = solved.at[k, :, part_rows(p), :]
        return remote(ref, ref, x_send.at[k, p, b], x_recv.at[k, p], {"row": diagonal_row() if b == len(bits) else flip(b)})

    def skips_stop(k, p):
        return k == count - 1 and len(bits) > 1 and p >= parts // 4

    def takes(k, p, b):
        go = row >= 0
        if b == len(bits):
            if not skips_stop(k, p):
                return None
            for low in range(2):
                go = jnp.logical_and(go, (row // 2**low) % 2 == (k // 2**low) % 2)
            return jnp.logical_and(go, diagonal_row() > k)
        skips = b == 0 and skips_stop(k, p)
        for low in range(2 if skips else b + 1):
            go = jnp.logical_and(go, (row // 2**low) % 2 == (k // 2**low) % 2)
        if b == 0:
            go = jnp.logical_and(go, flip(b) > k)
        return go

    def paths(k, p):
        return [b for b in bits + [len(bits)] if takes(k, p, b) is not None]

    def pass_on(k, p):
        for b in paths(k, p):

            @pl.when(takes(k, p, b))
            def _():
                send(k, p, b).start()

    half = max(1, parts // 2)

    def step(k, p):
        at = part_rows(p)

        @pl.when(row == k)
        def _():
            if k == 0 and p % half == 0:
                group = pl.ds(p * piece, half * piece)
                work[group, :] = product(split(work[group, :]), (inverse[0], inverse[1]))
            solved[k, 0, at, :], solved[k, 1, at, :] = split(work[at, :])
            pass_on(k, p)

        leaf = (row // 1) % 2 != k % 2

        @pl.when(jnp.logical_or(row > k, jnp.logical_and(row < k, jnp.logical_not(leaf))))
        def _():
            send(k, p, 0).wait_recv()
            pass_on(k, p)

        @pl.when(jnp.logical_and(row > k, row < count))
        def _():
            work[at, :] -= product((solved[k, 0, at, :], solved[k, 1, at, :]), (merged[k, 0], merged[k, 1]))

        @pl.when(row >= count)
        def _():
            work[at, :] -= dot_rows((solved[k, 0, at, :], solved[k, 1, at, :]), panels[k].astype(BF16))

    @pl.when(row < count)
    def _():
        for p in range(parts):
            for k in range(count):
                step(k, p)

    @pl.when(jnp.logical_and(row >= count, row % 2 == 0))
    def _():
        for k in range(count):
            for p in range(parts):
                step(k, p)

    @pl.when(jnp.logical_and(row >= count, row % 2 == 1))
    def _():
        pairs = [(k, p) for k in range(count) for p in range(parts)]
        for k, p in sorted(pairs, key=lambda pair: (pair[1] + parts // 2 * pair[0], -pair[0])):
            step(k, p)

    out_ref[...] = work[...].T

    for k in range(count):

        @pl.when(row > k)
        def _():
            for d in range(1, n_chip):
                far(k, d).wait_send()
            for d in range(n_chip):
                near(k, d).wait_send()

        @pl.when(row == k)
        def _():
            sent_own()
            if spread:
                for d in range(1, n_chip):
                    far_tile(d).wait_send()
                    near_tile(d).wait_send()

        for p in range(parts):
            for b in paths(k, p):

                @pl.when(takes(k, p, b))
                def _():
                    send(k, p, b).wait_send()


def body(n_row, n_rhs, factor, pivots, right_sides):
    factor = jnp.swapaxes(factor, 1, 2)
    count, slab, rows = factor.shape
    width = pivots.shape[1]
    columns = right_sides.shape[1]
    assert rows == width and n_rhs % CORES == 0
    parts = 4 if columns % 64 == 0 else 1
    n_chip = n_rhs // CORES
    n_bits = max(1, (n_row - 1).bit_length())
    wire = BF16 if slab % 16 == 0 else F32
    tile = min(LANES, width)
    vmem = pl.BlockSpec(memory_space=pltpu.VMEM)
    dma = pltpu.SemaphoreType.DMA
    return pl.pallas_call(
        functools.partial(kernel, n_row, n_rhs, parts),
        out_shape=jax.ShapeDtypeStruct(right_sides.shape, F32),
        in_specs=[pl.BlockSpec(memory_space=pltpu.HBM)] * 3,
        out_specs=vmem,
        scratch_shapes=[
            pltpu.VMEM((count, width, rows), wire),
            pltpu.VMEM((count, 2, columns, width), BF16),
            pltpu.VMEM((columns, rows), F32),
            pltpu.VMEM((2, width, width), BF16),
            pltpu.VMEM((width // tile, 2, tile, tile), BF16),
            pltpu.VMEM((count, 2, width, width), BF16),
            pltpu.VMEM(factor.shape, factor.dtype),
            pltpu.VMEM(pivots.shape, F32),
            pltpu.VMEM(right_sides.shape, F32),
            dma((count + 2,)),
            dma((count, n_chip)),
            dma((count, n_chip)),
            dma((count, n_chip)),
            dma((count, n_chip)),
            dma((n_chip,)),
            dma((n_chip,)),
            dma((n_chip,)),
            dma((n_chip,)),
            dma((count, parts, n_bits + 1)),
            dma((count, parts)),
        ],
        compiler_params=pltpu.CompilerParams(collective_id=0, has_side_effects=True, vmem_limit_bytes=40 * 2**20),
    )(*[pltpu.with_memory_space_constraint(array, pltpu.HBM) for array in (factor, pivots, right_sides)])


def solution(mesh):
    in_specs = (P(None, "row", "rhs"), P(), P("row", "rhs"))
    out_specs = P("row", "rhs")
    part = functools.partial(body, mesh.shape["row"], mesh.shape["rhs"])
    return jax.shard_map(part, mesh=mesh, in_specs=in_specs, out_specs=out_specs, check_vma=False)
```
